256 devices in a mesh: cam: 8 (over x, z_lo), pts: 32 (over y, z_hi, core).
Axes of the slice: x: 4, y: 4, z: 8 (z_hi: 4, z_lo: 2; z = z_hi * 2 + z_lo), core: 2. Of those that a mesh axis runs over, the one named last changes fastest.
Arguments:
- cam_jac: bfloat16 [12, 131072], P(None, ('cam', 'pts')), may hold values from -3 to 3
- pt_jac: bfloat16 [6, 131072], P(None, ('cam', 'pts')), may hold values from -6 to 6
- resid: float32 [2, 131072], P(None, ('cam', 'pts')), may hold values from -0.6 to 0.6
- obs_cam: int32 [131072], P(('cam', 'pts')), may hold values from 0 to 255, as said below
- obs_pt: int32 [131072], P(('cam', 'pts')), may hold values from 0 to 4095, as said below
- pairs: int32 [2, 16384], P(None, ('cam', 'pts')), may hold values from 0 to 255, as said below
- damping: float32 [1], replicated, may hold values from 1 to 8
Outputs:
- schur_blocks: float32 [36, 16384], P(None, ('cam', 'pts'))
- reduced_rhs: float32 [6, 256], P(None, 'cam')
The draws below stay inside these ranges and needn't reach their ends.
Inputs may be any that keep to these rules, and one draw needn't show every extreme that they name: `obs_cam`: observation block number g * 32 + b (aligned blocks of 512) holds only cameras g * 32 to (g + 1) * 32 - 1 and points b * 128 to (b + 1) * 128 - 1; no camera observes a point twice. `obs_pt`: see obs_cam: within aligned block g * 32 + b the points lie in range b. In aligned block g * 32 + b of 64 pairs, pairs[0] lies in cameras g * 32 to (g + 1) * 32 - 1 and pairs[1] in cameras b * 8 to (b + 1) * 8 - 1; pairs may repeat.
All inputs are finite; a program needn't handle non-finite values.
Results may differ from the reference program's by a relative error of at most 0.0016.
Values may be sent and summed in bfloat16 or wider, within the bound.
No kernel may reach another device: no remote copies, remote signals or barrier semaphores. Data moves between devices by JAX's collectives and lax.ppermute only.
A program may use at most 64 MiB of HBM per device.

```python
import math
import jax
import jax.numpy as jnp
from jax import lax

CAM_DEV = 32
PT_DEV = 128
OBS_DEV = 512
PAIR_DEV = 64
NCAM = 256
NPT = 4096
NOBS = 131072
NPAIRS = 16384
N_CAM = 8
N_PTS = 32


def observation_codes(key):
    blocks = N_CAM * N_PTS
    total = CAM_DEV * PT_DEV
    keys = jax.random.split(key, blocks)

    def one_block(block_key):
        rest = jax.random.permutation(block_key, total - 2)[:OBS_DEV - 2].astype(jnp.int32) + 1
        return jnp.concatenate([jnp.array([0, total - 1], jnp.int32), rest])
    codes = jax.vmap(one_block)(keys)
    order = jnp.arange(blocks, dtype=jnp.int32)
    return (codes, order // N_PTS, order % N_PTS)


def draw_obs_cam(key, part):
    codes, groups, ranges = observation_codes(key)
    return (groups[:, None] * CAM_DEV + codes // PT_DEV).reshape(-1)


def draw_obs_pt(key, part):
    codes, groups, ranges = observation_codes(key)
    return (ranges[:, None] * PT_DEV + codes % PT_DEV).reshape(-1)


def draw_pairs(key, part):
    key = jax.random.fold_in(key, 7)
    blocks = N_CAM * N_PTS
    width = CAM_DEV * N_CAM // N_PTS
    first_key, second_key = jax.random.split(key)
    first = jax.random.randint(first_key, (blocks, PAIR_DEV), 0, CAM_DEV)
    second = jax.random.randint(second_key, (blocks, PAIR_DEV), 0, width)
    first = first.at[:, 0].set(0).at[:, 1].set(CAM_DEV - 1)
    second = second.at[:, 0].set(0).at[:, 1].set(width - 1)
    order = jnp.arange(blocks, dtype=jnp.int32)
    groups = order // N_PTS
    ranges = order % N_PTS
    left = groups[:, None] * CAM_DEV + first
    right = ranges[:, None] * width + second
    return jnp.stack([left.reshape(-1), right.reshape(-1)]).astype(jnp.int32)


def steps_of(own_key, dims, cuts, least, high):
    gain = 1.0
    for axis_at, blocks in cuts:
        steps = jax.random.uniform(jax.random.fold_in(jax.random.fold_in(own_key, 6), axis_at), (blocks,), jnp.float32, least / len(cuts), high / len(cuts))
        gain = gain * jnp.repeat(jnp.exp(steps), dims[axis_at] // blocks).reshape((-1,) + (1,) * (len(dims) - 1 - axis_at))
    return gain


def bell_draw(rng, extent, scale, most, shards=(), kind=jnp.bfloat16):
    values = jax.random.normal(rng, extent, jnp.float32) * scale
    if len(shards) > 0:
        values = steps_of(rng, extent, shards, -0.22, 0.18) * values
    return jnp.clip(values, min=-most, max=most).astype(kind)


def setup_inputs(seed: int = 0) -> dict:
    key_list = jax.random.split(jax.random.key(seed), 8)
    cam_jac = bell_draw(key_list[0], (12, NOBS), 0.5, 3.0, ((1, 256),))
    pt_jac = bell_draw(key_list[1], (6, NOBS), 1.0, 6.0, ((1, 256),))
    resid = bell_draw(key_list[2], (2, NOBS), 0.1, 0.6, ((1, 256),), jnp.float32)
    obs_cam = draw_obs_cam(jax.random.fold_in(key_list[7], 71), 0)
    obs_pt = draw_obs_pt(jax.random.fold_in(key_list[7], 71), 0)
    pairs = draw_pairs(jax.random.fold_in(key_list[7], 71), 0)
    damping = jnp.clip(jnp.exp(jax.random.uniform(key_list[6], (1,), jnp.float32, math.log(1.0), math.log(8.0))), 1.0, 8.0)
    return {"cam_jac": cam_jac, "pt_jac": pt_jac, "resid": resid, "obs_cam": obs_cam, "obs_pt": obs_pt, "pairs": pairs, "damping": damping}


def point_parts(pt_jac, resid):
    jp = pt_jac.astype(jnp.float32)

    def entry(s, t):
        return jp[s] * jp[t] + jp[3 + s] * jp[3 + t]

    grads = [jp[s] * resid[0] + jp[3 + s] * resid[1] for s in range(3)]
    return jnp.stack([entry(0, 0), entry(0, 1), entry(0, 2), entry(1, 1), entry(1, 2), entry(2, 2)] + grads)


def invert(stats, lam):
    a = stats[0] + lam
    b = stats[1]
    c = stats[2]
    d = stats[3] + lam
    e = stats[4]
    f = stats[5] + lam
    m00 = d * f - e * e
    m01 = c * e - b * f
    m02 = b * e - c * d
    m11 = a * f - c * c
    m12 = b * c - a * e
    m22 = a * d - b * b
    det = a * m00 + b * m01 + c * m02
    return jnp.stack([m00, m01, m02, m11, m12, m22]) / det


def full_inverse(inv):
    return [[inv[0], inv[1], inv[2]], [inv[1], inv[3], inv[4]], [inv[2], inv[4], inv[5]]]


def solve_point(inv, grads):
    full = full_inverse(inv)
    return jnp.stack([full[r][0] * grads[0] + full[r][1] * grads[1] + full[r][2] * grads[2] for r in range(3)])


def couple(cam_jac, pt_jac):
    jc = cam_jac.astype(jnp.float32)
    jp = pt_jac.astype(jnp.float32)
    return jnp.stack([jc[k] * jp[s] + jc[6 + k] * jp[3 + s] for k in range(6) for s in range(3)])


def camera_terms(cam_jac, resid, coupling, y_obs):
    jc = cam_jac.astype(jnp.float32)
    rows = []
    for k in range(6):
        value = jc[k] * resid[0] + jc[6 + k] * resid[1]
        value = value - (coupling[k * 3] * y_obs[0] + coupling[k * 3 + 1] * y_obs[1] + coupling[k * 3 + 2] * y_obs[2])
        rows.append(value)
    return jnp.stack(rows)


def scale_obs(rounded, inv_obs):
    full = full_inverse(inv_obs)
    return jnp.stack([rounded[k * 3] * full[0][t] + rounded[k * 3 + 1] * full[1][t] + rounded[k * 3 + 2] * full[2][t] for k in range(6) for t in range(3)])


def place(values, cams, points, ncams, npoints):
    count = values.shape[1]
    rows = cams[None, :] * 6 + jnp.arange(6, dtype=jnp.int32)[:, None]
    comps = jnp.arange(3, dtype=jnp.int32)
    grid = jnp.zeros((ncams * 6, 3, npoints), jnp.float32)
    grid = grid.at[rows[:, None, :], comps[None, :, None], points[None, None, :]].add(values.reshape(6, 3, count))
    return grid.reshape(ncams, 6, 3 * npoints)


def reference(cam_jac, pt_jac, resid, obs_cam, obs_pt, pairs, damping):
    lam = damping[0]
    stats = point_parts(pt_jac, resid)
    totals = jax.ops.segment_sum(stats.T, obs_pt, num_segments=NPT).T
    inv = invert(totals, lam)
    y_pts = solve_point(inv, totals[6:])
    coupling = couple(cam_jac, pt_jac)
    inv_obs = inv[:, obs_pt]
    y_obs = y_pts[:, obs_pt]
    terms = camera_terms(cam_jac, resid, coupling, y_obs)
    reduced_rhs = jax.ops.segment_sum(terms.T, obs_cam, num_segments=NCAM).T
    rounded = coupling.astype(jnp.bfloat16)
    scaled = scale_obs(rounded.astype(jnp.float32), inv_obs).astype(jnp.bfloat16)
    blocks = N_CAM * N_PTS
    e_grid = rounded.astype(jnp.float32).reshape(18, N_CAM, N_PTS, OBS_DEV)
    f_grid = scaled.astype(jnp.float32).reshape(18, N_CAM, N_PTS, OBS_DEV)
    cam_grid = obs_cam.reshape(N_CAM, N_PTS, OBS_DEV)
    pt_grid = obs_pt.reshape(N_CAM, N_PTS, OBS_DEV)
    first = pairs[0].reshape(blocks, PAIR_DEV)
    second = pairs[1].reshape(blocks, PAIR_DEV)

    def one_range(total, index):
        e_vals = lax.dynamic_index_in_dim(e_grid, index, 2, False).reshape(18, N_CAM * OBS_DEV)
        f_vals = lax.dynamic_index_in_dim(f_grid, index, 2, False).reshape(18, N_CAM * OBS_DEV)
        cams = lax.dynamic_index_in_dim(cam_grid, index, 1, False).reshape(-1)
        points = lax.dynamic_index_in_dim(pt_grid, index, 1, False).reshape(-1) - index * PT_DEV
        design = place(e_vals, cams, points, NCAM, PT_DEV)
        weighted = place(f_vals, cams, points, NCAM, PT_DEV)

        def one_block(ids):
            left = weighted[ids[0]]
            right = design[ids[1]]
            return jnp.einsum("qkc,qlc->qkl", left, right, precision=lax.Precision.HIGHEST)

        return total + lax.map(one_block, (first, second)), None

    start = jnp.zeros((blocks, PAIR_DEV, 6, 6), jnp.float32)
    total, unused = lax.scan(one_range, start, jnp.arange(N_PTS, dtype=jnp.int32))
    schur_blocks = total.reshape(NPAIRS, 36).T
    return schur_blocks, reduced_rhs
```

```python
import jax
import jax.numpy as jnp
from jax import lax
from jax.experimental import pallas as pl
from jax.experimental.pallas import tpu as pltpu
from jax.sharding import PartitionSpec as P

CAM_DEV = 32
PT_DEV = 128
OBS_DEV = 512
PAIR_DEV = 64
N_CAM = 8
N_PTS = 32
SLICE = 8
ROWS = 80
F32 = jnp.float32
BF16 = jnp.bfloat16


def split3(x):
    hi = x.astype(BF16)
    rest = x - hi.astype(F32)
    mid = rest.astype(BF16)
    low = (rest - mid.astype(F32)).astype(BF16)
    return hi.astype(F32), mid.astype(F32), low.astype(F32)


def nt(a, b):
    return lax.dot_general(a, b, (((1,), (1,)), ((), ())), preferred_element_type=F32)


def nn(a, b):
    return lax.dot_general(a, b, (((1,), (0,)), ((), ())), preferred_element_type=F32)


def pack_kernel(cj_ref, pj_ref, res_ref, cam_ref, pt_ref, out_ref):
    cj = cj_ref[...].astype(F32)
    pj = pj_ref[...].astype(F32)
    res = res_ref[...]
    high = res.astype(BF16).astype(F32)
    low = res - high
    cam = (cam_ref[...] & (CAM_DEV - 1)).astype(F32)
    pt = (pt_ref[...] & (PT_DEV - 1)).astype(F32)
    left = jnp.concatenate([cj[:6], high, cj[6:], low], axis=0).astype(BF16)
    right = jnp.concatenate([pj, cam, pt], axis=0)
    right = jnp.concatenate([right[:, :256], right[:, 256:]], axis=0).astype(BF16)
    for g in range(N_CAM):
        out_ref[g, :, :OBS_DEV] = left
        out_ref[g, :, OBS_DEV:] = right


def unpack(m):
    x = m[:, :OBS_DEV].astype(F32)
    y = m[:, OBS_DEV:].astype(F32)
    return x[:8], x[8:], jnp.concatenate([y[:8], y[8:]], axis=1)


def spread(x0, x1, pj, hots):
    blocks = []
    for s in range(3):
        e = x0 * pj[s : s + 1] + x1 * pj[3 + s : 4 + s]
        for hot in hots:
            for k in range(6):
                blocks.append(hot * e[k : k + 1])
    return blocks


def main_kernel(ranges, subs, id_ref, lam_ref, *refs):
    gat_refs = refs[:ranges]
    out_ref, d_ref, w_ref = refs[ranges:]
    group = id_ref[0]
    core = id_ref[1]
    lam = lam_ref[0]
    iota8 = lax.broadcasted_iota(jnp.int32, (8, OBS_DEV), 0)
    iota32 = lax.broadcasted_iota(jnp.int32, (CAM_DEV, OBS_DEV), 0).astype(F32)
    iotap = lax.broadcasted_iota(jnp.int32, (PT_DEV, OBS_DEV), 0).astype(F32)
    step = 4 // subs
    firsts = [(iota8 + ((h * step + core) if subs < 4 else h) * SLICE).astype(F32) for h in range(subs)]
    per = subs * 48
    rhs = jnp.zeros((8, CAM_DEV), F32)

    for r in range(ranges):
        gat_ref = gat_refs[r]

        def one_group(g, totals):
            x0, x1, pj = unpack(gat_ref[g])
            cam = pj[6:7]
            pt = pj[7:8]
            hots = [jnp.where(f == cam, 1.0, 0.0) for f in firsts]
            blocks = spread(x0, x1, pj, hots)
            res = x0 + x1
            jp = [pj[i : i + 1] for i in range(6)]
            r0 = res[6:7]
            r1 = res[7:8]
            stats = [jp[s] * jp[t] + jp[3 + s] * jp[3 + t] for s, t in
                     ((0, 0), (0, 1), (0, 2), (1, 1), (1, 2), (2, 2))]
            stats = stats + [jp[s] * r0 + jp[3 + s] * r1 for s in range(3)]
            stats = stats + [jnp.zeros((7, OBS_DEV), F32)]
            rows = jnp.concatenate(stats, axis=0)
            left = jnp.concatenate(blocks + list(split3(rows)), axis=0).astype(BF16)
            pt_hot = jnp.where(iotap == pt, 1.0, 0.0).astype(BF16)
            grid = nt(left, pt_hot)
            for s in range(3):
                at = (r * 3 + s) * PT_DEV
                d_ref[g, :, at : at + PT_DEV] = grid[s * per : (s + 1) * per].astype(BF16)
            top = 3 * per
            return totals + (grid[top : top + 16] + grid[top + 16 : top + 32] + grid[top + 32 : top + 48])

        totals = lax.fori_loop(0, N_CAM, one_group, jnp.zeros((16, PT_DEV), F32))

        a = totals[0:1] + lam
        b = totals[1:2]
        c = totals[2:3]
        d = totals[3:4] + lam
        e = totals[4:5]
        f = totals[5:6] + lam
        m00 = d * f - e * e
        m01 = c * e - b * f
        m02 = b * e - c * d
        m11 = a * f - c * c
        m12 = b * c - a * e
        m22 = a * d - b * b
        det = a * m00 + b * m01 + c * m02
        i00, i01, i02, i11, i12, i22 = [m / det for m in (m00, m01, m02, m11, m12, m22)]
        full = [[i00, i01, i02], [i01, i11, i12], [i02, i12, i22]]
        grads = [totals[6 + s : 7 + s] for s in range(3)]
        y = [full[q][0] * grads[0] + full[q][1] * grads[1] + full[q][2] * grads[2] for q in range(3)]

        x0, x1, pj = unpack(gat_ref[group])
        cam = pj[6:7]
        pt = pj[7:8]
        cam_hot = jnp.where(iota32 == cam, 1.0, 0.0)
        pt_hot = jnp.where(iotap == pt, 1.0, 0.0).astype(BF16)
        left = jnp.concatenate(spread(x0, x1, pj, [cam_hot]), axis=0).astype(BF16)
        grid = nt(left, pt_hot)
        for t in range(3):
            value = grid[:192] * full[0][t] + grid[192:384] * full[1][t] + grid[384:] * full[2][t]
            at = (r * 3 + t) * PT_DEV
            w_ref[:, at : at + PT_DEV] = value.astype(BF16)

        y8 = jnp.concatenate(y + [jnp.zeros((5, PT_DEV), F32)], axis=0)
        y_obs = nn(jnp.concatenate(split3(y8), axis=0).astype(BF16), pt_hot)
        y_obs = y_obs[:8] + y_obs[8:16] + y_obs[16:24]
        res = x0 + x1
        left0 = res[6:7] - (pj[0:1] * y_obs[0:1] + pj[1:2] * y_obs[1:2] + pj[2:3] * y_obs[2:3])
        left1 = res[7:8] - (pj[3:4] * y_obs[0:1] + pj[4:5] * y_obs[1:2] + pj[5:6] * y_obs[2:3])
        terms = x0 * left0 + x1 * left1
        part = nt(jnp.concatenate(split3(terms), axis=0).astype(BF16), cam_hot.astype(BF16))
        rhs = rhs + (part[:8] + part[8:16] + part[16:24])

    rhs_high = rhs.astype(BF16).astype(F32)
    rhs_rows = jnp.concatenate([rhs_high, rhs - rhs_high, jnp.zeros((8, 64), F32)], axis=1)
    w = w_ref[...]

    def one_product(g, carry):
        product = nt(d_ref[g], w)
        for h in range(subs):
            block = product[h * 48 : (h + 1) * 48]
            tail = block[:, 128:192]
            tail = jnp.concatenate([tail[:24], tail[24:]], axis=1)
            whole = jnp.concatenate([block[:, :128], tail, rhs_rows], axis=0)
            out_ref[g * subs + h] = whole.astype(BF16)
        return carry

    lax.fori_loop(0, N_CAM, one_product, 0)


def last_kernel(got_ref, pairs_ref, schur_ref, rhs_ref):
    total = got_ref[0].astype(F32)
    for i in range(1, got_ref.shape[0]):
        total = total + got_ref[i].astype(F32)
    rhs = total[72:80]
    rhs_ref[...] = rhs[:6, :CAM_DEV] + rhs[:6, CAM_DEV : 2 * CAM_DEV]
    tail = total[48:72]
    tail = jnp.concatenate([tail[:, :64], tail[:, 64:]], axis=0)
    tail = jnp.concatenate([tail, jnp.zeros((48, 64), F32)], axis=1)
    pairs = pairs_ref[...]
    left = (pairs[0:1] & (CAM_DEV - 1))
    right = (pairs[1:2] & (SLICE - 1))
    lefts = jnp.concatenate([left + CAM_DEV * k for k in range(4)], axis=1)
    rights = jnp.concatenate([right] * 6, axis=1)
    pick = jnp.where(
        lax.broadcasted_iota(jnp.int32, (128, 256), 0) == lefts, 1.0, 0.0
    ).astype(BF16)
    first = nn(jnp.concatenate(split3(total[:48]), axis=0).astype(BF16), pick)
    second = nn(jnp.concatenate(split3(tail), axis=0).astype(BF16), pick[:, :128])
    z = jnp.concatenate([first, second], axis=1)
    z = z[:48] + z[48:96] + z[96:]
    keep = lax.broadcasted_iota(jnp.int32, (SLICE, 384), 0) == rights
    rows = [
        jnp.sum(jnp.where(keep, z[l * 8 : (l + 1) * 8], 0.0), axis=0, keepdims=True) for l in range(6)
    ]
    rows = jnp.concatenate(rows, axis=0)
    for k in range(6):
        schur_ref[k * 6 : (k + 1) * 6, :] = rows[:, k * PAIR_DEV : (k + 1) * PAIR_DEV]


def local(cam_jac, pt_jac, resid, obs_cam, obs_pt, pairs, damping):
    group = lax.axis_index("cam")
    block = lax.axis_index("pts")
    smem = pl.BlockSpec(memory_space=pltpu.SMEM)
    vmem = pl.BlockSpec(memory_space=pltpu.VMEM)
    packed = pl.pallas_call(
        pack_kernel,
        out_shape=jax.ShapeDtypeStruct((N_CAM, 16, 768), BF16),
        in_specs=[vmem] * 5,
        out_specs=vmem,
    )(cam_jac, pt_jac, resid, obs_cam.reshape(1, OBS_DEV), obs_pt.reshape(1, OBS_DEV))
    gathered = lax.all_to_all(packed, "cam", 0, 0)
    ids = jnp.stack([group, block % 2]).astype(jnp.int32)
    if MERGE:
        other = lax.ppermute(gathered, "pts", [(i, i ^ 1) for i in range(N_PTS)])
        gats = [gathered, other]
        ranges, subs = 2, 2
    else:
        gats = [gathered]
        ranges, subs = 1, 4
    sends = N_CAM * subs
    send = pl.pallas_call(
        lambda *refs: main_kernel(ranges, subs, *refs),
        out_shape=jax.ShapeDtypeStruct((sends, ROWS, 128), BF16),
        in_specs=[smem, smem] + [vmem] * ranges,
        out_specs=vmem,
        scratch_shapes=[
            pltpu.VMEM((N_CAM, subs * 48, ranges * 3 * PT_DEV), BF16),
            pltpu.VMEM((192, ranges * 3 * PT_DEV), BF16),
        ],
    )(ids, damping, *gats)
    if MERGE:
        same = [[2 * i + c for i in range(N_PTS // 2)] for c in range(2)]
        got = lax.all_to_all(send, "pts", 0, 0, axis_index_groups=same)
    else:
        got = lax.all_to_all(send, "pts", 0, 0)
    return pl.pallas_call(
        last_kernel,
        out_shape=(
            jax.ShapeDtypeStruct((36, PAIR_DEV), F32),
            jax.ShapeDtypeStruct((6, CAM_DEV), F32),
        ),
        in_specs=[vmem, vmem],
        out_specs=(vmem, vmem),
    )(got, pairs)


MERGE = False


def solution(mesh):
    return jax.shard_map(
        local,
        mesh=mesh,
        in_specs=(
            P(None, ("cam", "pts")),
            P(None, ("cam", "pts")),
            P(None, ("cam", "pts")),
            P(("cam", "pts")),
            P(("cam", "pts")),
            P(None, ("cam", "pts")),
            P(),
        ),
        out_specs=(P(None, ("cam", "pts")), P(None, "cam")),
        check_vma=False,
    )
```

```python
import jax
import jax.numpy as jnp
from jax import lax
from jax.experimental import pallas as pl
from jax.experimental.pallas import tpu as pltpu
from jax.sharding import PartitionSpec as P

CAM_DEV = 32
PT_DEV = 128
OBS_DEV = 512
PAIR_DEV = 64
N_CAM = 8
N_PTS = 32
SLICE = 8
ROWS = 80
F32 = jnp.float32
BF16 = jnp.bfloat16


def split3(x):
    hi = x.astype(BF16)
    rest = x - hi.astype(F32)
    mid = rest.astype(BF16)
    low = (rest - mid.astype(F32)).astype(BF16)
    return hi.astype(F32), mid.astype(F32), low.astype(F32)


def nt(a, b):
    return lax.dot_general(a, b, (((1,), (1,)), ((), ())), preferred_element_type=F32)


def nn(a, b):
    return lax.dot_general(a, b, (((1,), (0,)), ((), ())), preferred_element_type=F32)


def pack_kernel(cj_ref, pj_ref, res_ref, cam_ref, pt_ref, out_ref):
    cj = cj_ref[...].astype(F32)
    pj = pj_ref[...].astype(F32)
    res = res_ref[...]
    high = res.astype(BF16).astype(F32)
    low = res - high
    cam = (cam_ref[...] & (CAM_DEV - 1)).astype(F32)
    pt = (pt_ref[...] & (PT_DEV - 1)).astype(F32)
    left = jnp.concatenate([cj[:6], high, cj[6:], low], axis=0).astype(BF16)
    right = jnp.concatenate([pj, cam, pt], axis=0)
    right = jnp.concatenate([right[:, :256], right[:, 256:]], axis=0).astype(BF16)
    for g in range(N_CAM):
        out_ref[g, :, :OBS_DEV] = left
        out_ref[g, :, OBS_DEV:] = right


def unpack(m):
    x = m[:, :OBS_DEV].astype(F32)
    y = m[:, OBS_DEV:].astype(F32)
    return x[:8], x[8:], jnp.concatenate([y[:8], y[8:]], axis=1)


def spread(x0, x1, pj, hots):
    blocks = []
    for s in range(3):
        e = x0 * pj[s : s + 1] + x1 * pj[3 + s : 4 + s]
        for hot in hots:
            for k in range(6):
                blocks.append(hot * e[k : k + 1])
    return blocks


def main_kernel(ranges, subs, lam_ref, *refs):
    gat_refs = refs[:ranges]
    out_ref, d_ref, w_ref = refs[ranges:]
    group = lax.axis_index("cam")
    core = lax.axis_index("pts") % 2
    lam = lam_ref[...]
    iota8 = lax.broadcasted_iota(jnp.int32, (8, OBS_DEV), 0)
    iota32 = lax.broadcasted_iota(jnp.int32, (CAM_DEV, OBS_DEV), 0).astype(F32)
    iotap = lax.broadcasted_iota(jnp.int32, (PT_DEV, OBS_DEV), 0).astype(F32)
    step = 4 // subs
    firsts = [(iota8 + ((h * step + core) if subs < 4 else h) * SLICE).astype(F32) for h in range(subs)]
    per = subs * 48
    rhs = jnp.zeros((8, CAM_DEV), F32)

    for r in range(ranges):
        gat_ref = gat_refs[r]

        def one_group(g, totals):
            x0, x1, pj = unpack(gat_ref[g])
            cam = pj[6:7]
            pt = pj[7:8]
            hots = [jnp.where(f == cam, 1.0, 0.0) for f in firsts]
            blocks = spread(x0, x1, pj, hots)
            res = x0 + x1
            jp = [pj[i : i + 1] for i in range(6)]
            r0 = res[6:7]
            r1 = res[7:8]
            stats = [jp[s] * jp[t] + jp[3 + s] * jp[3 + t] for s, t in
                     ((0, 0), (0, 1), (0, 2), (1, 1), (1, 2), (2, 2))]
            stats = stats + [jp[s] * r0 + jp[3 + s] * r1 for s in range(3)]
            stats = stats + [jnp.zeros((7, OBS_DEV), F32)]
            rows = jnp.concatenate(stats, axis=0)
            left = jnp.concatenate(blocks + list(split3(rows)), axis=0).astype(BF16)
            pt_hot = jnp.where(iotap == pt, 1.0, 0.0).astype(BF16)
            grid = nt(left, pt_hot)
            for s in range(3):
                at = (r * 3 + s) * PT_DEV
                d_ref[g, :, at : at + PT_DEV] = grid[s * per : (s + 1) * per].astype(BF16)
            top = 3 * per
            return totals + (grid[top : top + 16] + grid[top + 16 : top + 32] + grid[top + 32 : top + 48])

        totals = lax.fori_loop(0, N_CAM, one_group, jnp.zeros((16, PT_DEV), F32), unroll=4)

        a = totals[0:1] + lam
        b = totals[1:2]
        c = totals[2:3]
        d = totals[3:4] + lam
        e = totals[4:5]
        f = totals[5:6] + lam
        m00 = d * f - e * e
        m01 = c * e - b * f
        m02 = b * e - c * d
        m11 = a * f - c * c
        m12 = b * c - a * e
        m22 = a * d - b * b
        det = a * m00 + b * m01 + c * m02
        i00, i01, i02, i11, i12, i22 = [m / det for m in (m00, m01, m02, m11, m12, m22)]
        full = [[i00, i01, i02], [i01, i11, i12], [i02, i12, i22]]
        grads = [totals[6 + s : 7 + s] for s in range(3)]
        y = [full[q][0] * grads[0] + full[q][1] * grads[1] + full[q][2] * grads[2] for q in range(3)]

        x0, x1, pj = unpack(gat_ref[group])
        cam = pj[6:7]
        pt = pj[7:8]
        cam_hot = jnp.where(iota32 == cam, 1.0, 0.0)
        pt_hot = jnp.where(iotap == pt, 1.0, 0.0).astype(BF16)
        left = jnp.concatenate(spread(x0, x1, pj, [cam_hot]), axis=0).astype(BF16)
        grid = nt(left, pt_hot)
        for t in range(3):
            value = grid[:192] * full[0][t] + grid[192:384] * full[1][t] + grid[384:] * full[2][t]
            at = (r * 3 + t) * PT_DEV
            w_ref[:, at : at + PT_DEV] = value.astype(BF16)

        y8 = jnp.concatenate(y + [jnp.zeros((5, PT_DEV), F32)], axis=0)
        y_obs = nn(jnp.concatenate(split3(y8), axis=0).astype(BF16), pt_hot)
        y_obs = y_obs[:8] + y_obs[8:16] + y_obs[16:24]
        res = x0 + x1
        left0 = res[6:7] - (pj[0:1] * y_obs[0:1] + pj[1:2] * y_obs[1:2] + pj[2:3] * y_obs[2:3])
        left1 = res[7:8] - (pj[3:4] * y_obs[0:1] + pj[4:5] * y_obs[1:2] + pj[5:6] * y_obs[2:3])
        terms = x0 * left0 + x1 * left1
        part = nt(jnp.concatenate(split3(terms), axis=0).astype(BF16), cam_hot.astype(BF16))
        rhs = rhs + (part[:8] + part[8:16] + part[16:24])

    rhs_high = rhs.astype(BF16).astype(F32)
    rhs_rows = jnp.concatenate([rhs_high, rhs - rhs_high, jnp.zeros((8, 64), F32)], axis=1)
    w = w_ref[...]

    def one_product(g, carry):
        product = nt(d_ref[g], w)
        for h in range(subs):
            block = product[h * 48 : (h + 1) * 48]
            tail = block[:, 128:192]
            tail = jnp.concatenate([tail[:24], tail[24:]], axis=1)
            whole = jnp.concatenate([block[:, :128], tail, rhs_rows], axis=0)
            out_ref[g * subs + h] = whole.astype(BF16)
        return carry

    lax.fori_loop(0, N_CAM, one_product, 0, unroll=4)


def last_kernel(got_ref, pairs_ref, schur_ref, rhs_ref):
    total = got_ref[0].astype(F32)
    for i in range(1, got_ref.shape[0]):
        total = total + got_ref[i].astype(F32)
    rhs = total[72:80]
    rhs_ref[...] = rhs[:6, :CAM_DEV] + rhs[:6, CAM_DEV : 2 * CAM_DEV]
    tail = total[48:72]
    tail = jnp.concatenate([tail[:, :64], tail[:, 64:]], axis=0)
    tail = jnp.concatenate([tail, jnp.zeros((48, 64), F32)], axis=1)
    pairs = pairs_ref[...]
    left = (pairs[0:1] & (CAM_DEV - 1))
    right = (pairs[1:2] & (SLICE - 1))
    lefts = jnp.concatenate([left + CAM_DEV * k for k in range(4)], axis=1)
    rights = jnp.concatenate([right] * 6, axis=1)
    pick = jnp.where(
        lax.broadcasted_iota(jnp.int32, (128, 256), 0) == lefts, 1.0, 0.0
    ).astype(BF16)
    first = nn(jnp.concatenate(split3(total[:48]), axis=0).astype(BF16), pick)
    second = nn(jnp.concatenate(split3(tail), axis=0).astype(BF16), pick[:, :128])
    z = jnp.concatenate([first, second], axis=1)
    z = z[:48] + z[48:96] + z[96:]
    keep = lax.broadcasted_iota(jnp.int32, (SLICE, 384), 0) == rights
    rows = [
        jnp.sum(jnp.where(keep, z[l * 8 : (l + 1) * 8], 0.0), axis=0, keepdims=True) for l in range(6)
    ]
    rows = jnp.concatenate(rows, axis=0)
    for k in range(6):
        schur_ref[k * 6 : (k + 1) * 6, :] = rows[:, k * PAIR_DEV : (k + 1) * PAIR_DEV]


def local(cam_jac, pt_jac, resid, obs_cam, obs_pt, pairs, damping):
    vmem = pl.BlockSpec(memory_space=pltpu.VMEM)
    packed = pl.pallas_call(
        pack_kernel,
        out_shape=jax.ShapeDtypeStruct((N_CAM, 16, 768), BF16),
        in_specs=[vmem] * 5,
        out_specs=vmem,
    )(cam_jac, pt_jac, resid, obs_cam.reshape(1, OBS_DEV), obs_pt.reshape(1, OBS_DEV))
    gathered = lax.all_to_all(packed, "cam", 0, 0)
    if MERGE:
        other = lax.ppermute(gathered, "pts", [(i, i ^ 1) for i in range(N_PTS)])
        gats = [gathered, other]
        ranges, subs = 2, 2
    else:
        gats = [gathered]
        ranges, subs = 1, 4
    sends = N_CAM * subs
    send = pl.pallas_call(
        lambda *refs: main_kernel(ranges, subs, *refs),
        out_shape=jax.ShapeDtypeStruct((sends, ROWS, 128), BF16),
        in_specs=[vmem] + [vmem] * ranges,
        out_specs=vmem,
        compiler_params=SMALL,
        scratch_shapes=[
            pltpu.VMEM((N_CAM, subs * 48, ranges * 3 * PT_DEV), BF16),
            pltpu.VMEM((192, ranges * 3 * PT_DEV), BF16),
        ],
    )(damping.reshape(1, 1), *gats)
    if MERGE:
        same = [[2 * i + c for i in range(N_PTS // 2)] for c in range(2)]
        got = lax.all_to_all(send, "pts", 0, 0, axis_index_groups=same)
    else:
        got = lax.all_to_all(send, "pts", 0, 0)
    return pl.pallas_call(
        last_kernel,
        out_shape=(
            jax.ShapeDtypeStruct((36, PAIR_DEV), F32),
            jax.ShapeDtypeStruct((6, CAM_DEV), F32),
        ),
        in_specs=[vmem, vmem],
        out_specs=(vmem, vmem),
        compiler_params=SMALL,
    )(got, pairs)


MERGE = True
SMALL = pltpu.CompilerParams(vmem_limit_bytes=16 * 1024 * 1024)


def solution(mesh):
    return jax.shard_map(
        local,
        mesh=mesh,
        in_specs=(
            P(None, ("cam", "pts")),
            P(None, ("cam", "pts")),
            P(None, ("cam", "pts")),
            P(("cam", "pts")),
            P(("cam", "pts")),
            P(None, ("cam", "pts")),
            P(),
        ),
        out_specs=(P(None, ("cam", "pts")), P(None, "cam")),
        check_vma=False,
    )
```

```python
import jax
import jax.numpy as jnp
from jax import lax
from jax.experimental import pallas as pl
from jax.experimental.pallas import tpu as pltpu
from jax.sharding import PartitionSpec as P

CAM_DEV = 32
PT_DEV = 128
OBS_DEV = 512
PAIR_DEV = 64
N_CAM = 8
N_PTS = 32
SLICE = 8
ROWS = 80
F32 = jnp.float32
BF16 = jnp.bfloat16
UNROLL = 4
SMALL = pltpu.CompilerParams(vmem_limit_bytes=16 * 1024 * 1024)
SCRATCH = [pltpu.VMEM((N_CAM, 96, 768), BF16), pltpu.VMEM((192, 768), BF16)]


def split3(x):
    hi = x.astype(BF16)
    rest = x - hi.astype(F32)
    mid = rest.astype(BF16)
    low = (rest - mid.astype(F32)).astype(BF16)
    return hi.astype(F32), mid.astype(F32), low.astype(F32)


def nt(a, b):
    return lax.dot_general(a, b, (((1,), (1,)), ((), ())), preferred_element_type=F32)


def nn(a, b):
    return lax.dot_general(a, b, (((1,), (0,)), ((), ())), preferred_element_type=F32)


def pack_kernel(cj_ref, pj_ref, res_ref, cam_ref, pt_ref, out_ref):
    cj = cj_ref[...].astype(F32)
    pj = pj_ref[...].astype(F32)
    res = res_ref[...]
    high = res.astype(BF16).astype(F32)
    low = res - high
    cam = (cam_ref[...] & (CAM_DEV - 1)).astype(F32)
    pt = (pt_ref[...] & (PT_DEV - 1)).astype(F32)
    left = jnp.concatenate([cj[:6], high, cj[6:], low], axis=0).astype(BF16)
    right = jnp.concatenate([pj, cam, pt], axis=0)
    right = jnp.concatenate([right[:, :256], right[:, 256:]], axis=0).astype(BF16)
    for g in range(N_CAM):
        out_ref[g, :, :OBS_DEV] = left
        out_ref[g, :, OBS_DEV:] = right


def unpack(m):
    x = m[:, :OBS_DEV].astype(F32)
    y = m[:, OBS_DEV:].astype(F32)
    return x[:8], x[8:], jnp.concatenate([y[:8], y[8:]], axis=1)


def spread(x0, x1, pj, hots):
    blocks = []
    for s in range(3):
        e = x0 * pj[s : s + 1] + x1 * pj[3 + s : 4 + s]
        for hot in hots:
            for k in range(6):
                blocks.append(hot * e[k : k + 1])
    return blocks


def stat_rows(x0, x1, pj):
    res = x0 + x1
    jp = [pj[i : i + 1] for i in range(6)]
    r0 = res[6:7]
    r1 = res[7:8]
    rows = [jp[s] * jp[t] + jp[3 + s] * jp[3 + t] for s, t in
            ((0, 0), (0, 1), (0, 2), (1, 1), (1, 2), (2, 2))]
    rows = rows + [jp[s] * r0 + jp[3 + s] * r1 for s in range(3)]
    last = jnp.concatenate(list(split3(rows[8])) + [jnp.zeros((5, OBS_DEV), F32)], axis=0)
    return list(split3(jnp.concatenate(rows[:8], axis=0))) + [last]


def point_inverse(totals, lam):
    a = totals[0] + lam
    b = totals[1]
    c = totals[2]
    d = totals[3] + lam
    e = totals[4]
    f = totals[5] + lam
    m00 = d * f - e * e
    m01 = c * e - b * f
    m02 = b * e - c * d
    m11 = a * f - c * c
    m12 = b * c - a * e
    m22 = a * d - b * b
    det = a * m00 + b * m01 + c * m02
    i00, i01, i02, i11, i12, i22 = [m / det for m in (m00, m01, m02, m11, m12, m22)]
    full = [[i00, i01, i02], [i01, i11, i12], [i02, i12, i22]]
    y = [full[q][0] * totals[6] + full[q][1] * totals[7] + full[q][2] * totals[8] for q in range(3)]
    return full, y


def main_kernel(lam_ref, gat0_ref, gat1_ref, out_ref, d_ref, w_ref):
    group = lax.axis_index("cam")
    core = lax.axis_index("pts") % 2
    gat_refs = (gat0_ref, gat1_ref)
    iota8 = lax.broadcasted_iota(jnp.int32, (SLICE, OBS_DEV), 0) + core * SLICE
    firsts = [(iota8 + h * 2 * SLICE).astype(F32) for h in range(2)]
    iota32 = lax.broadcasted_iota(jnp.int32, (CAM_DEV, OBS_DEV), 0).astype(F32)
    iotap = lax.broadcasted_iota(jnp.int32, (PT_DEV, OBS_DEV), 0).astype(F32)

    def one_group(g, totals):
        after = []
        for r in range(2):
            x0, x1, pj = unpack(gat_refs[r][g])
            hots = [jnp.where(f == pj[6:7], 1.0, 0.0) for f in firsts]
            left = spread(x0, x1, pj, hots) + stat_rows(x0, x1, pj)
            left = jnp.concatenate(left, axis=0).astype(BF16)
            pt_hot = jnp.where(iotap == pj[7:8], 1.0, 0.0).astype(BF16)
            grid = nt(left, pt_hot)
            for s in range(3):
                at = (r * 3 + s) * PT_DEV
                d_ref[g, :, at : at + PT_DEV] = grid[s * 96 : (s + 1) * 96].astype(BF16)
            after.append(totals[r] + grid[288:320])
        return tuple(after)

    zero = jnp.zeros((32, PT_DEV), F32)
    totals = lax.fori_loop(0, N_CAM, one_group, (zero, zero), unroll=UNROLL)
    totals = jnp.concatenate(totals, axis=1)
    eight = totals[:8] + totals[8:16] + totals[16:24]
    ninth = totals[24:25] + totals[25:26] + totals[26:27]
    full, y = point_inverse([eight[i : i + 1] for i in range(8)] + [ninth], lam_ref[...])

    rhs = jnp.zeros((8, CAM_DEV), F32)
    for r in range(2):
        mine = slice(r * PT_DEV, (r + 1) * PT_DEV)
        x0, x1, pj = unpack(gat_refs[r][group])
        cam_hot = jnp.where(iota32 == pj[6:7], 1.0, 0.0)
        pt_hot = jnp.where(iotap == pj[7:8], 1.0, 0.0).astype(BF16)
        left = jnp.concatenate(spread(x0, x1, pj, [cam_hot]), axis=0).astype(BF16)
        grid = nt(left, pt_hot)
        for t in range(3):
            value = (grid[:192] * full[0][t][:, mine] + grid[192:384] * full[1][t][:, mine]
                     + grid[384:] * full[2][t][:, mine])
            at = (r * 3 + t) * PT_DEV
            w_ref[:, at : at + PT_DEV] = value.astype(BF16)
        y8 = jnp.concatenate([v[:, mine] for v in y] + [jnp.zeros((5, PT_DEV), F32)], axis=0)
        y_obs = nn(jnp.concatenate(split3(y8), axis=0).astype(BF16), pt_hot)
        y_obs = y_obs[:8] + y_obs[8:16] + y_obs[16:24]
        res = x0 + x1
        left0 = res[6:7] - (pj[0:1] * y_obs[0:1] + pj[1:2] * y_obs[1:2] + pj[2:3] * y_obs[2:3])
        left1 = res[7:8] - (pj[3:4] * y_obs[0:1] + pj[4:5] * y_obs[1:2] + pj[5:6] * y_obs[2:3])
        terms = x0 * left0 + x1 * left1
        part = nt(jnp.concatenate(split3(terms), axis=0).astype(BF16), cam_hot.astype(BF16))
        rhs = rhs + (part[:8] + part[8:16] + part[16:24])

    rhs_high = rhs.astype(BF16).astype(F32)
    rhs_rows = jnp.concatenate([rhs_high, rhs - rhs_high, jnp.zeros((8, 64), F32)], axis=1)
    product = nt(d_ref[...].reshape(N_CAM * 96, 768), w_ref[...])
    for i in range(2 * N_CAM):
        block = product[i * 48 : (i + 1) * 48]
        tail = block[:, 128:192]
        tail = jnp.concatenate([tail[:24], tail[24:]], axis=1)
        whole = jnp.concatenate([block[:, :128], tail, rhs_rows], axis=0)
        out_ref[i] = whole.astype(BF16)


def last_kernel(got_ref, pairs_ref, schur_ref, rhs_ref):
    total = got_ref[0].astype(F32)
    for i in range(1, got_ref.shape[0]):
        total = total + got_ref[i].astype(F32)
    rhs = total[72:80]
    rhs_ref[...] = rhs[:6, :CAM_DEV] + rhs[:6, CAM_DEV : 2 * CAM_DEV]
    tail = total[48:72]
    tail = jnp.concatenate([tail[:, :64], tail[:, 64:]], axis=0)
    tail = jnp.concatenate([tail, jnp.zeros((48, 64), F32)], axis=1)
    pairs = pairs_ref[...]
    left = (pairs[0:1] & (CAM_DEV - 1))
    right = (pairs[1:2] & (SLICE - 1))
    lefts = jnp.concatenate([left + CAM_DEV * k for k in range(4)], axis=1)
    rights = jnp.concatenate([right] * 6, axis=1)
    pick = jnp.where(
        lax.broadcasted_iota(jnp.int32, (128, 256), 0) == lefts, 1.0, 0.0
    ).astype(BF16)
    first = nn(jnp.concatenate(split3(total[:48]), axis=0).astype(BF16), pick)
    second = nn(jnp.concatenate(split3(tail), axis=0).astype(BF16), pick[:, :128])
    z = jnp.concatenate([first, second], axis=1)
    z = z[:48] + z[48:96] + z[96:]
    keep = lax.broadcasted_iota(jnp.int32, (SLICE, 384), 0) == rights
    rows = [
        jnp.sum(jnp.where(keep, z[l * 8 : (l + 1) * 8], 0.0), axis=0, keepdims=True) for l in range(6)
    ]
    rows = jnp.concatenate(rows, axis=0)
    for k in range(6):
        schur_ref[k * 6 : (k + 1) * 6, :] = rows[:, k * PAIR_DEV : (k + 1) * PAIR_DEV]


def local(cam_jac, pt_jac, resid, obs_cam, obs_pt, pairs, damping):
    vmem = pl.BlockSpec(memory_space=pltpu.VMEM)
    packed = pl.pallas_call(
        pack_kernel,
        out_shape=jax.ShapeDtypeStruct((N_CAM, 16, 768), BF16),
        in_specs=[vmem] * 5,
        out_specs=vmem,
    )(cam_jac, pt_jac, resid, obs_cam.reshape(1, OBS_DEV), obs_pt.reshape(1, OBS_DEV))
    gathered = lax.all_to_all(packed, "cam", 0, 0)
    other = lax.ppermute(gathered, "pts", [(i, i ^ 1) for i in range(N_PTS)])
    send = pl.pallas_call(
        main_kernel,
        out_shape=jax.ShapeDtypeStruct((2 * N_CAM, ROWS, 128), BF16),
        in_specs=[vmem] * 3,
        out_specs=vmem,
        compiler_params=SMALL,
        scratch_shapes=SCRATCH,
    )(damping.reshape(1, 1), gathered, other)
    same = [[2 * i + c for i in range(N_PTS // 2)] for c in range(2)]
    got = lax.all_to_all(send, "pts", 0, 0, axis_index_groups=same)
    return pl.pallas_call(
        last_kernel,
        out_shape=(
            jax.ShapeDtypeStruct((36, PAIR_DEV), F32),
            jax.ShapeDtypeStruct((6, CAM_DEV), F32),
        ),
        in_specs=[vmem, vmem],
        out_specs=(vmem, vmem),
        compiler_params=SMALL,
    )(got, pairs)


def solution(mesh):
    return jax.shard_map(
        local,
        mesh=mesh,
        in_specs=(
            P(None, ("cam", "pts")),
            P(None, ("cam", "pts")),
            P(None, ("cam", "pts")),
            P(("cam", "pts")),
            P(("cam", "pts")),
            P(None, ("cam", "pts")),
            P(),
        ),
        out_specs=(P(None, ("cam", "pts")), P(None, "cam")),
        check_vma=False,
    )
```

```python
import jax
import jax.numpy as jnp
from jax import lax
from jax.experimental import pallas as pl
from jax.experimental.pallas import tpu as pltpu
from jax.sharding import PartitionSpec as P

CAM_DEV = 32
PT_DEV = 128
OBS_DEV = 512
PAIR_DEV = 64
N_CAM = 8
N_PTS = 32
SLICE = 8
ROWS = 80
F32 = jnp.float32
BF16 = jnp.bfloat16
UNROLL = 8
SMALL = pltpu.CompilerParams(vmem_limit_bytes=16 * 1024 * 1024)
SCRATCH = [pltpu.VMEM((N_CAM, 96, 384), BF16), pltpu.VMEM((2, 192, 384), BF16)]


def split3(x):
    hi = x.astype(BF16)
    rest = x - hi.astype(F32)
    mid = rest.astype(BF16)
    low = (rest - mid.astype(F32)).astype(BF16)
    return hi.astype(F32), mid.astype(F32), low.astype(F32)


def nt(a, b):
    return lax.dot_general(a, b, (((1,), (1,)), ((), ())), preferred_element_type=F32)


def nn(a, b):
    return lax.dot_general(a, b, (((1,), (0,)), ((), ())), preferred_element_type=F32)


def pack_kernel(cj_ref, pj_ref, res_ref, cam_ref, pt_ref, out_ref):
    cj = cj_ref[...].astype(F32)
    pj = pj_ref[...].astype(F32)
    res = res_ref[...]
    high = res.astype(BF16).astype(F32)
    low = res - high
    cam = (cam_ref[...] & (CAM_DEV - 1)).astype(F32)
    pt = (pt_ref[...] & (PT_DEV - 1)).astype(F32)
    left = jnp.concatenate([cj[:6], high, cj[6:], low], axis=0).astype(BF16)
    right = jnp.concatenate([pj, cam, pt], axis=0)
    right = jnp.concatenate([right[:, :256], right[:, 256:]], axis=0).astype(BF16)
    for g in range(N_CAM):
        out_ref[g, :, :OBS_DEV] = left
        out_ref[g, :, OBS_DEV:] = right


def unpack(m):
    x = m.astype(F32)
    x1 = jnp.concatenate([x[6:12], x[12:14] + x[14:16]], axis=0)
    return x[:8], x1, x[16:24]


def spread(x0, x1, pj, hots):
    blocks = []
    for s in range(3):
        e = x0 * pj[s : s + 1] + x1 * pj[3 + s : 4 + s]
        for hot in hots:
            for k in range(6):
                blocks.append(hot * e[k : k + 1])
    return blocks


def stat_rows(x0, x1, pj):
    jp = [pj[i : i + 1] for i in range(6)]
    r0 = x1[6:7]
    r1 = x1[7:8]
    rows = [jp[s] * jp[t] + jp[3 + s] * jp[3 + t] for s, t in
            ((0, 0), (0, 1), (0, 2), (1, 1), (1, 2), (2, 2))]
    rows = rows + [jp[s] * r0 + jp[3 + s] * r1 for s in range(3)]
    last = jnp.concatenate(list(split3(rows[8])) + [jnp.zeros((5, OBS_DEV), F32)], axis=0)
    return list(split3(jnp.concatenate(rows[:8], axis=0))) + [last]


def point_inverse(totals, lam):
    a = totals[0] + lam
    b = totals[1]
    c = totals[2]
    d = totals[3] + lam
    e = totals[4]
    f = totals[5] + lam
    m00 = d * f - e * e
    m01 = c * e - b * f
    m02 = b * e - c * d
    m11 = a * f - c * c
    m12 = b * c - a * e
    m22 = a * d - b * b
    det = a * m00 + b * m01 + c * m02
    i00, i01, i02, i11, i12, i22 = [m / det for m in (m00, m01, m02, m11, m12, m22)]
    full = [[i00, i01, i02], [i01, i11, i12], [i02, i12, i22]]
    y = [full[q][0] * totals[6] + full[q][1] * totals[7] + full[q][2] * totals[8] for q in range(3)]
    return full, y


def cells(pj, iotac):
    half = jnp.where(pj[6:7] >= 16.0, 1.0, 0.0)
    cell_hot = jnp.where(iotac == pj[7:8] + half * PT_DEV, 1.0, 0.0).astype(BF16)
    return pj[6:7] - half * 16.0, cell_hot


def build_range(gat_ref, d_ref):
    core = lax.axis_index("pts") % 2
    first = (lax.broadcasted_iota(jnp.int32, (SLICE, OBS_DEV), 0) + core * SLICE).astype(F32)
    iotac = lax.broadcasted_iota(jnp.int32, (2 * PT_DEV, OBS_DEV), 0).astype(F32)

    def one_group(g, totals):
        x0, x1, pj = unpack(gat_ref[g])
        low, cell_hot = cells(pj, iotac)
        hot = jnp.where(first == low, 1.0, 0.0)
        left = spread(x0, x1, pj, [hot]) + stat_rows(x0, x1, pj)
        grid = nt(jnp.concatenate(left, axis=0).astype(BF16), cell_hot)
        for s in range(3):
            part = grid[s * 48 : (s + 1) * 48].astype(BF16)
            d_ref[g, :48, s * PT_DEV : (s + 1) * PT_DEV] = part[:, :PT_DEV]
            d_ref[g, 48:, s * PT_DEV : (s + 1) * PT_DEV] = part[:, PT_DEV:]
        return totals + (grid[144:176, :PT_DEV] + grid[144:176, PT_DEV:])

    return lax.fori_loop(0, N_CAM, one_group, jnp.zeros((32, PT_DEV), F32), unroll=UNROLL)


def first_kernel(gat_ref, d_ref, totals_ref):
    totals_ref[...] = build_range(gat_ref, d_ref)


def main_kernel(lam_ref, totals_ref, d0_ref, gat0_ref, gat1_ref, out_ref, d1_ref, w_ref):
    group = lax.axis_index("cam")
    gat_refs = (gat0_ref, gat1_ref)
    iota16 = lax.broadcasted_iota(jnp.int32, (16, OBS_DEV), 0).astype(F32)
    iotac = lax.broadcasted_iota(jnp.int32, (2 * PT_DEV, OBS_DEV), 0).astype(F32)
    totals = jnp.concatenate([totals_ref[...], build_range(gat1_ref, d1_ref)], axis=1)
    eight = totals[:8] + totals[8:16] + totals[16:24]
    ninth = totals[24:25] + totals[25:26] + totals[26:27]
    full, y = point_inverse([eight[i : i + 1] for i in range(8)] + [ninth], lam_ref[...])

    rhs = jnp.zeros((8, CAM_DEV), F32)
    for r in range(2):
        mine = slice(r * PT_DEV, (r + 1) * PT_DEV)
        x0, x1, pj = unpack(gat_refs[r][group])
        low, cell_hot = cells(pj, iotac)
        hot = jnp.where(iota16 == low, 1.0, 0.0)
        left = jnp.concatenate(spread(x0, x1, pj, [hot]), axis=0).astype(BF16)
        grid = nt(left, cell_hot)
        for t in range(3):
            scale = [jnp.concatenate([full[s][t][:, mine]] * 2, axis=1) for s in range(3)]
            value = (grid[:96] * scale[0] + grid[96:192] * scale[1] + grid[192:] * scale[2]).astype(BF16)
            at = t * PT_DEV
            for k in range(6):
                for h in range(2):
                    w_ref[r, k * 32 + h * 16 : k * 32 + (h + 1) * 16, at : at + PT_DEV] = (
                        value[k * 16 : (k + 1) * 16, h * PT_DEV : (h + 1) * PT_DEV])
        y8 = jnp.concatenate([v[:, mine] for v in y] + [jnp.zeros((5, PT_DEV), F32)], axis=0)
        y8 = jnp.concatenate([y8, y8], axis=1)
        y_obs = nn(jnp.concatenate(split3(y8), axis=0).astype(BF16), cell_hot)
        y_obs = y_obs[:8] + y_obs[8:16] + y_obs[16:24]
        left0 = x1[6:7] - (pj[0:1] * y_obs[0:1] + pj[1:2] * y_obs[1:2] + pj[2:3] * y_obs[2:3])
        left1 = x1[7:8] - (pj[3:4] * y_obs[0:1] + pj[4:5] * y_obs[1:2] + pj[5:6] * y_obs[2:3])
        terms = x0 * left0 + x1 * left1
        cam_hot = jnp.where(iotac[:CAM_DEV] == pj[6:7], 1.0, 0.0).astype(BF16)
        part = nt(jnp.concatenate(split3(terms), axis=0).astype(BF16), cam_hot)
        rhs = rhs + (part[:8] + part[8:16] + part[16:24])

    rhs_high = rhs.astype(BF16).astype(F32)
    rhs_rows = jnp.concatenate([rhs_high, rhs - rhs_high, jnp.zeros((8, 64), F32)], axis=1)
    product = nt(d0_ref[...].reshape(N_CAM * 96, 384), w_ref[0])
    product = product + nt(d1_ref[...].reshape(N_CAM * 96, 384), w_ref[1])
    for i in range(2 * N_CAM):
        block = product[i * 48 : (i + 1) * 48]
        tail = block[:, 128:192]
        tail = jnp.concatenate([tail[:24], tail[24:]], axis=1)
        whole = jnp.concatenate([block[:, :128], tail, rhs_rows], axis=0)
        out_ref[i] = whole.astype(BF16)


def last_kernel(got_ref, pairs_ref, schur_ref, rhs_ref):
    total = got_ref[0].astype(F32)
    for i in range(1, got_ref.shape[0]):
        total = total + got_ref[i].astype(F32)
    rhs = total[72:80]
    rhs_ref[...] = rhs[:6, :CAM_DEV] + rhs[:6, CAM_DEV : 2 * CAM_DEV]
    tail = total[48:72]
    tail = jnp.concatenate([tail[:, :64], tail[:, 64:]], axis=0)
    tail = jnp.concatenate([tail, jnp.zeros((48, 64), F32)], axis=1)
    pairs = pairs_ref[...]
    left = (pairs[0:1] & (CAM_DEV - 1))
    right = (pairs[1:2] & (SLICE - 1))
    lefts = jnp.concatenate([left + CAM_DEV * k for k in range(4)], axis=1)
    rights = jnp.concatenate([right] * 6, axis=1)
    pick = jnp.where(
        lax.broadcasted_iota(jnp.int32, (128, 256), 0) == lefts, 1.0, 0.0
    ).astype(BF16)
    first = nn(jnp.concatenate(split3(total[:48]), axis=0).astype(BF16), pick)
    second = nn(jnp.concatenate(split3(tail), axis=0).astype(BF16), pick[:, :128])
    z = jnp.concatenate([first, second], axis=1)
    z = z[:48] + z[48:96] + z[96:]
    keep = lax.broadcasted_iota(jnp.int32, (SLICE, 384), 0) == rights
    rows = [
        jnp.sum(jnp.where(keep, z[l * 8 : (l + 1) * 8], 0.0), axis=0, keepdims=True) for l in range(6)
    ]
    rows = jnp.concatenate(rows, axis=0)
    for k in range(6):
        schur_ref[k * 6 : (k + 1) * 6, :] = rows[:, k * PAIR_DEV : (k + 1) * PAIR_DEV]


def local(cam_jac, pt_jac, resid, obs_cam, obs_pt, pairs, damping):
    vmem = pl.BlockSpec(memory_space=pltpu.VMEM)
    def rows(x, at):
        return jnp.pad(x, ((at, 24 - at - x.shape[0]), (0, 0)))

    cell = lax.broadcasted_iota(jnp.int32, (24, OBS_DEV), 0) * OBS_DEV
    cell = cell + lax.broadcasted_iota(jnp.int32, (24, OBS_DEV), 1)

    def code(x, mask, at):
        keep = jnp.where((cell >= at * OBS_DEV) & (cell < (at + 1) * OBS_DEV), mask, 0)
        return lax.broadcast_in_dim(x, (24, OBS_DEV), (1,)) & keep

    cam = code(obs_cam, CAM_DEV - 1, 22)
    pt = code(obs_pt, PT_DEV - 1, 23)
    second = rows(resid, 14)
    packed = ((rows(cam_jac, 0) + rows(pt_jac, 16)).astype(F32) + (cam + pt).astype(F32) + rows(resid, 12)
              + (second - lax.reduce_precision(second, 8, 7))).astype(BF16)
    packed = jnp.broadcast_to(packed[None], (N_CAM, 24, OBS_DEV))
    gathered = lax.all_to_all(packed, "cam", 0, 0)
    other = lax.ppermute(gathered, "pts", [(i, i ^ 1) for i in range(N_PTS)])
    d0, totals = pl.pallas_call(
        first_kernel,
        out_shape=(
            jax.ShapeDtypeStruct((N_CAM, 96, 384), BF16),
            jax.ShapeDtypeStruct((32, PT_DEV), F32),
        ),
        in_specs=[vmem],
        out_specs=(vmem, vmem),
        compiler_params=SMALL,
        cost_estimate=pl.CostEstimate(flops=10**9, bytes_accessed=10**6, transcendentals=0),
    )(gathered)
    send = pl.pallas_call(
        main_kernel,
        out_shape=jax.ShapeDtypeStruct((2 * N_CAM, ROWS, 128), BF16),
        in_specs=[vmem] * 5,
        out_specs=vmem,
        compiler_params=SMALL,
        scratch_shapes=SCRATCH,
    )(damping.reshape(1, 1), totals, d0, gathered, other)
    same = [[2 * i + c for i in range(N_PTS // 2)] for c in range(2)]
    got = lax.all_to_all(send, "pts", 0, 0, axis_index_groups=same)
    return pl.pallas_call(
        last_kernel,
        out_shape=(
            jax.ShapeDtypeStruct((36, PAIR_DEV), F32),
            jax.ShapeDtypeStruct((6, CAM_DEV), F32),
        ),
        in_specs=[vmem, vmem],
        out_specs=(vmem, vmem),
        compiler_params=SMALL,
    )(got, pairs)


def solution(mesh):
    return jax.shard_map(
        local,
        mesh=mesh,
        in_specs=(
            P(None, ("cam", "pts")),
            P(None, ("cam", "pts")),
            P(None, ("cam", "pts")),
            P(("cam", "pts")),
            P(("cam", "pts")),
            P(None, ("cam", "pts")),
            P(),
        ),
        out_specs=(P(None, ("cam", "pts")), P(None, "cam")),
        check_vma=False,
    )
```

```python
import jax
import jax.numpy as jnp
from jax import lax
from jax.experimental import pallas as pl
from jax.experimental.pallas import tpu as pltpu
from jax.sharding import PartitionSpec as P

CAM_DEV = 32
PT_DEV = 128
OBS_DEV = 512
PAIR_DEV = 64
N_CAM = 8
N_PTS = 32
SLICE = 8
ROWS = 80
F32 = jnp.float32
BF16 = jnp.bfloat16
UNROLL = 8
SMALL = pltpu.CompilerParams(vmem_limit_bytes=16 * 1024 * 1024)
SCRATCH = [pltpu.VMEM((N_CAM, 96, 384), BF16), pltpu.VMEM((2, 192, 384), BF16)]


def split3(x):
    hi = x.astype(BF16)
    rest = x - hi.astype(F32)
    mid = rest.astype(BF16)
    low = (rest - mid.astype(F32)).astype(BF16)
    return hi.astype(F32), mid.astype(F32), low.astype(F32)


def nt(a, b):
    return lax.dot_general(a, b, (((1,), (1,)), ((), ())), preferred_element_type=F32)


def nn(a, b):
    return lax.dot_general(a, b, (((1,), (0,)), ((), ())), preferred_element_type=F32)


def pack_kernel(cj_ref, pj_ref, res_ref, cam_ref, pt_ref, out_ref):
    cj = cj_ref[...].astype(F32)
    pj = pj_ref[...].astype(F32)
    res = res_ref[...]
    high = res.astype(BF16).astype(F32)
    low = res - high
    cam = (cam_ref[...] & (CAM_DEV - 1)).astype(F32)
    pt = (pt_ref[...] & (PT_DEV - 1)).astype(F32)
    left = jnp.concatenate([cj[:6], high, cj[6:], low], axis=0).astype(BF16)
    right = jnp.concatenate([pj, cam, pt], axis=0)
    right = jnp.concatenate([right[:, :256], right[:, 256:]], axis=0).astype(BF16)
    for g in range(N_CAM):
        out_ref[g, :, :OBS_DEV] = left
        out_ref[g, :, OBS_DEV:] = right


def unpack(m):
    x = m.astype(F32)
    x1 = jnp.concatenate([x[6:12], x[12:14] + x[14:16]], axis=0)
    return x[:8], x1, x[16:24]


def spread(x0, x1, pj, hots):
    blocks = []
    for s in range(3):
        e = x0 * pj[s : s + 1] + x1 * pj[3 + s : 4 + s]
        for hot in hots:
            for k in range(6):
                blocks.append(hot * e[k : k + 1])
    return blocks


def stat_rows(x0, x1, pj):
    jp = [pj[i : i + 1] for i in range(6)]
    r0 = x1[6:7]
    r1 = x1[7:8]
    rows = [jp[s] * jp[t] + jp[3 + s] * jp[3 + t] for s, t in
            ((0, 0), (0, 1), (0, 2), (1, 1), (1, 2), (2, 2))]
    rows = rows + [jp[s] * r0 + jp[3 + s] * r1 for s in range(3)]
    last = jnp.concatenate(list(split3(rows[8])) + [jnp.zeros((5, OBS_DEV), F32)], axis=0)
    return list(split3(jnp.concatenate(rows[:8], axis=0))) + [last]


def point_inverse(totals, lam):
    a = totals[0] + lam
    b = totals[1]
    c = totals[2]
    d = totals[3] + lam
    e = totals[4]
    f = totals[5] + lam
    m00 = d * f - e * e
    m01 = c * e - b * f
    m02 = b * e - c * d
    m11 = a * f - c * c
    m12 = b * c - a * e
    m22 = a * d - b * b
    det = a * m00 + b * m01 + c * m02
    i00, i01, i02, i11, i12, i22 = [m / det for m in (m00, m01, m02, m11, m12, m22)]
    full = [[i00, i01, i02], [i01, i11, i12], [i02, i12, i22]]
    y = [full[q][0] * totals[6] + full[q][1] * totals[7] + full[q][2] * totals[8] for q in range(3)]
    return full, y


def cells(pj, iotac):
    half = jnp.where(pj[6:7] >= 16.0, 1.0, 0.0)
    cell_hot = jnp.where(iotac == pj[7:8] + half * PT_DEV, 1.0, 0.0).astype(BF16)
    return pj[6:7] - half * 16.0, cell_hot


def build_range(gat_ref, d_ref):
    core = lax.axis_index("pts") % 2
    first = (lax.broadcasted_iota(jnp.int32, (SLICE, OBS_DEV), 0) + core * SLICE).astype(F32)
    iotac = lax.broadcasted_iota(jnp.int32, (2 * PT_DEV, OBS_DEV), 0).astype(F32)

    def one_group(g, totals):
        x0, x1, pj = unpack(gat_ref[g])
        low, cell_hot = cells(pj, iotac)
        hot = jnp.where(first == low, 1.0, 0.0)
        left = spread(x0, x1, pj, [hot]) + stat_rows(x0, x1, pj)
        grid = nt(jnp.concatenate(left, axis=0).astype(BF16), cell_hot)
        for s in range(3):
            part = grid[s * 48 : (s + 1) * 48].astype(BF16)
            d_ref[g, :48, s * PT_DEV : (s + 1) * PT_DEV] = part[:, :PT_DEV]
            d_ref[g, 48:, s * PT_DEV : (s + 1) * PT_DEV] = part[:, PT_DEV:]
        return totals + (grid[144:176, :PT_DEV] + grid[144:176, PT_DEV:])

    return lax.fori_loop(0, N_CAM, one_group, jnp.zeros((32, PT_DEV), F32), unroll=UNROLL)


def first_kernel(gat_ref, pairs_ref, d_ref, totals_ref, near_ref):
    near_ref[...] = pairs_ref[...]
    totals_ref[...] = build_range(gat_ref, d_ref)


def fit(x):
    most = jnp.max(jnp.max(jnp.abs(x), axis=0, keepdims=True), axis=1, keepdims=True)
    power = jnp.floor(jnp.log2(jnp.maximum(most, 1e-30)))
    return power, jnp.exp2(14.0 - power)


def main_kernel(lam_ref, totals_ref, d0_ref, gat0_ref, gat1_ref, out_ref, d1_ref, w_ref):
    group = lax.axis_index("cam")
    gat_refs = (gat0_ref, gat1_ref)
    iota16 = lax.broadcasted_iota(jnp.int32, (16, OBS_DEV), 0).astype(F32)
    iotac = lax.broadcasted_iota(jnp.int32, (2 * PT_DEV, OBS_DEV), 0).astype(F32)
    totals = jnp.concatenate([totals_ref[...], build_range(gat1_ref, d1_ref)], axis=1)
    eight = totals[:8] + totals[8:16] + totals[16:24]
    ninth = totals[24:25] + totals[25:26] + totals[26:27]
    full, y = point_inverse([eight[i : i + 1] for i in range(8)] + [ninth], lam_ref[...])

    rhs = jnp.zeros((8, CAM_DEV), F32)
    for r in range(2):
        mine = slice(r * PT_DEV, (r + 1) * PT_DEV)
        x0, x1, pj = unpack(gat_refs[r][group])
        low, cell_hot = cells(pj, iotac)
        hot = jnp.where(iota16 == low, 1.0, 0.0)
        left = jnp.concatenate(spread(x0, x1, pj, [hot]), axis=0).astype(BF16)
        grid = nt(left, cell_hot)
        for t in range(3):
            scale = [jnp.concatenate([full[s][t][:, mine]] * 2, axis=1) for s in range(3)]
            value = (grid[:96] * scale[0] + grid[96:192] * scale[1] + grid[192:] * scale[2]).astype(BF16)
            at = t * PT_DEV
            for k in range(6):
                for h in range(2):
                    w_ref[r, k * 32 + h * 16 : k * 32 + (h + 1) * 16, at : at + PT_DEV] = (
                        value[k * 16 : (k + 1) * 16, h * PT_DEV : (h + 1) * PT_DEV])
        y8 = jnp.concatenate([v[:, mine] for v in y] + [jnp.zeros((5, PT_DEV), F32)], axis=0)
        y8 = jnp.concatenate([y8, y8], axis=1)
        y_obs = nn(jnp.concatenate(split3(y8), axis=0).astype(BF16), cell_hot)
        y_obs = y_obs[:8] + y_obs[8:16] + y_obs[16:24]
        left0 = x1[6:7] - (pj[0:1] * y_obs[0:1] + pj[1:2] * y_obs[1:2] + pj[2:3] * y_obs[2:3])
        left1 = x1[7:8] - (pj[3:4] * y_obs[0:1] + pj[4:5] * y_obs[1:2] + pj[5:6] * y_obs[2:3])
        terms = x0 * left0 + x1 * left1
        cam_hot = jnp.where(iotac[:CAM_DEV] == pj[6:7], 1.0, 0.0).astype(BF16)
        part = nt(jnp.concatenate(split3(terms), axis=0).astype(BF16), cam_hot)
        rhs = rhs + (part[:8] + part[8:16] + part[16:24])

    product = nt(d0_ref[...].reshape(N_CAM * 96, 384), w_ref[0])
    product = product + nt(d1_ref[...].reshape(N_CAM * 96, 384), w_ref[1])
    power, scale = fit(product)
    rhs_power, rhs_scale = fit(rhs)
    rhs = rhs * rhs_scale
    rhs_high = rhs.astype(BF16).astype(F32)
    rhs_rows = jnp.concatenate(
        [rhs_high, rhs - rhs_high, jnp.broadcast_to(power, (8, 32)), jnp.broadcast_to(rhs_power, (8, 32))],
        axis=1,
    )
    for i in range(2 * N_CAM):
        block = product[i * 48 : (i + 1) * 48] * scale
        tail = block[:, 128:192]
        tail = jnp.concatenate([tail[:24], tail[24:]], axis=1)
        out_ref[i] = jnp.concatenate([block[:, :128], tail, rhs_rows], axis=0)


def last_kernel(got_ref, pairs_ref, schur_ref, rhs_ref):
    total = jnp.zeros((72, 128), F32)
    rhs = jnp.zeros((8, CAM_DEV), F32)
    for i in range(got_ref.shape[0]):
        part = got_ref[i].astype(F32)
        scales = jnp.exp2(part[72:73] - 14.0)
        total = total + part[:72] * scales[:, 64:65]
        rhs = rhs + (part[72:80, :32] + part[72:80, 32:64]) * scales[:, 96:97]
    rhs_ref[...] = rhs[:6]
    tail = total[48:72]
    tail = jnp.concatenate([tail[:, :64], tail[:, 64:]], axis=0)
    tail = jnp.concatenate([tail, jnp.zeros((48, 64), F32)], axis=1)
    pairs = pairs_ref[...]
    left = (pairs[0:1] & (CAM_DEV - 1))
    right = (pairs[1:2] & (SLICE - 1))
    lefts = jnp.concatenate([left + CAM_DEV * k for k in range(4)], axis=1)
    rights = jnp.concatenate([right] * 6, axis=1)
    pick = jnp.where(
        lax.broadcasted_iota(jnp.int32, (128, 256), 0) == lefts, 1.0, 0.0
    ).astype(BF16)
    first = nn(jnp.concatenate(split3(total[:48]), axis=0).astype(BF16), pick)
    second = nn(jnp.concatenate(split3(tail), axis=0).astype(BF16), pick[:, :128])
    z = jnp.concatenate([first, second], axis=1)
    z = z[:48] + z[48:96] + z[96:]
    keep = lax.broadcasted_iota(jnp.int32, (SLICE, 384), 0) == rights
    rows = [
        jnp.sum(jnp.where(keep, z[l * 8 : (l + 1) * 8], 0.0), axis=0, keepdims=True) for l in range(6)
    ]
    rows = jnp.concatenate(rows, axis=0)
    for k in range(6):
        schur_ref[k * 6 : (k + 1) * 6, :] = rows[:, k * PAIR_DEV : (k + 1) * PAIR_DEV]


def local(cam_jac, pt_jac, resid, obs_cam, obs_pt, pairs, damping):
    vmem = pl.BlockSpec(memory_space=pltpu.VMEM)
    def rows(x, at):
        return jnp.pad(x, ((at, 24 - at - x.shape[0]), (0, 0)))

    cell = lax.broadcasted_iota(jnp.int32, (24, OBS_DEV), 0) * OBS_DEV
    cell = cell + lax.broadcasted_iota(jnp.int32, (24, OBS_DEV), 1)

    def code(x, mask, at):
        keep = jnp.where((cell >= at * OBS_DEV) & (cell < (at + 1) * OBS_DEV), mask, 0)
        return lax.broadcast_in_dim(x, (24, OBS_DEV), (1,)) & keep

    cam = code(obs_cam, CAM_DEV - 1, 22)
    pt = code(obs_pt, PT_DEV - 1, 23)
    second = rows(resid, 14)
    packed = ((rows(cam_jac, 0) + rows(pt_jac, 16)).astype(F32) + (cam + pt).astype(F32) + rows(resid, 12)
              + (second - lax.reduce_precision(second, 8, 7))).astype(BF16)
    packed = jnp.broadcast_to(packed[None], (N_CAM, 24, OBS_DEV))
    gathered = lax.all_to_all(packed, "cam", 0, 0)
    other = lax.ppermute(gathered, "pts", [(i, i ^ 1) for i in range(N_PTS)])
    d0, totals, near = pl.pallas_call(
        first_kernel,
        out_shape=(
            jax.ShapeDtypeStruct((N_CAM, 96, 384), BF16),
            jax.ShapeDtypeStruct((32, PT_DEV), F32),
            jax.ShapeDtypeStruct((2, PAIR_DEV), jnp.int32),
        ),
        in_specs=[vmem] * 2,
        out_specs=(vmem,) * 3,
        compiler_params=SMALL,
        cost_estimate=pl.CostEstimate(flops=10**9, bytes_accessed=10**6, transcendentals=0),
    )(gathered, pairs)
    send = pl.pallas_call(
        main_kernel,
        out_shape=jax.ShapeDtypeStruct((2 * N_CAM, ROWS, 128), F32),
        in_specs=[vmem] * 5,
        out_specs=vmem,
        compiler_params=SMALL,
        scratch_shapes=SCRATCH,
    )(damping.reshape(1, 1), totals, d0, gathered, other)
    same = [[2 * i + c for i in range(N_PTS // 2)] for c in range(2)]
    got = lax.all_to_all(send.astype(jnp.float16), "pts", 0, 0, axis_index_groups=same).astype(F32)
    return pl.pallas_call(
        last_kernel,
        out_shape=(
            jax.ShapeDtypeStruct((36, PAIR_DEV), F32),
            jax.ShapeDtypeStruct((6, CAM_DEV), F32),
        ),
        in_specs=[vmem, vmem],
        out_specs=(vmem, vmem),
        compiler_params=SMALL,
    )(got, near)


def solution(mesh):
    return jax.shard_map(
        local,
        mesh=mesh,
        in_specs=(
            P(None, ("cam", "pts")),
            P(None, ("cam", "pts")),
            P(None, ("cam", "pts")),
            P(("cam", "pts")),
            P(("cam", "pts")),
            P(None, ("cam", "pts")),
            P(),
        ),
        out_specs=(P(None, ("cam", "pts")), P(None, "cam")),
        check_vma=False,
    )
```

```python
import jax
import jax.numpy as jnp
from jax import lax
from jax.experimental import pallas as pl
from jax.experimental.pallas import tpu as pltpu
from jax.sharding import PartitionSpec as P

CAM_DEV = 32
PT_DEV = 128
OBS_DEV = 512
PAIR_DEV = 64
N_CAM = 8
N_PTS = 32
SLICE = 8
ROWS = 80
F32 = jnp.float32
BF16 = jnp.bfloat16
UNROLL = 8
ORDERS = ([4 * (y if z % 2 == 0 else 3 - y) + z for z in range(4) for y in range(4)], [4 * (y if z % 2 == 0 else 3 - y) + z for z in range(4) for y in range(4)][::-1], [4 * (y if z % 2 == 0 else 3 - y) + z for z in range(4) for y in range(4)][::-1], [4 * (y if z % 2 == 0 else 3 - y) + z for z in range(4) for y in range(4)])
SMALL = pltpu.CompilerParams(vmem_limit_bytes=16 * 1024 * 1024)
SCRATCH = [pltpu.VMEM((N_CAM, 96, 384), BF16), pltpu.VMEM((2, 192, 384), BF16)]


def split3(x):
    hi = x.astype(BF16)
    rest = x - hi.astype(F32)
    mid = rest.astype(BF16)
    low = (rest - mid.astype(F32)).astype(BF16)
    return hi.astype(F32), mid.astype(F32), low.astype(F32)


def nt(a, b):
    return lax.dot_general(a, b, (((1,), (1,)), ((), ())), preferred_element_type=F32)


def nn(a, b):
    return lax.dot_general(a, b, (((1,), (0,)), ((), ())), preferred_element_type=F32)


def pack_kernel(cj_ref, pj_ref, res_ref, cam_ref, pt_ref, out_ref):
    cj = cj_ref[...].astype(F32)
    pj = pj_ref[...].astype(F32)
    res = res_ref[...]
    high = res.astype(BF16).astype(F32)
    low = res - high
    cam = (cam_ref[...] & (CAM_DEV - 1)).astype(F32)
    pt = (pt_ref[...] & (PT_DEV - 1)).astype(F32)
    left = jnp.concatenate([cj[:6], high, cj[6:], low], axis=0).astype(BF16)
    right = jnp.concatenate([pj, cam, pt], axis=0)
    right = jnp.concatenate([right[:, :256], right[:, 256:]], axis=0).astype(BF16)
    for g in range(N_CAM):
        out_ref[g, :, :OBS_DEV] = left
        out_ref[g, :, OBS_DEV:] = right


def unpack(m):
    x = m.astype(F32)
    x1 = jnp.concatenate([x[6:12], x[12:14] + x[14:16]], axis=0)
    return x[:8], x1, x[16:24]


def spread(x0, x1, pj, hots):
    blocks = []
    for s in range(3):
        e = x0 * pj[s : s + 1] + x1 * pj[3 + s : 4 + s]
        for hot in hots:
            for k in range(6):
                blocks.append(hot * e[k : k + 1])
    return blocks


def stat_rows(x0, x1, pj):
    jp = [pj[i : i + 1] for i in range(6)]
    r0 = x1[6:7]
    r1 = x1[7:8]
    rows = [jp[s] * jp[t] + jp[3 + s] * jp[3 + t] for s, t in
            ((0, 0), (0, 1), (0, 2), (1, 1), (1, 2), (2, 2))]
    rows = rows + [jp[s] * r0 + jp[3 + s] * r1 for s in range(3)]
    last = jnp.concatenate(list(split3(rows[8])) + [jnp.zeros((5, OBS_DEV), F32)], axis=0)
    return list(split3(jnp.concatenate(rows[:8], axis=0))) + [last]


def point_inverse(totals, lam):
    a = totals[0] + lam
    b = totals[1]
    c = totals[2]
    d = totals[3] + lam
    e = totals[4]
    f = totals[5] + lam
    m00 = d * f - e * e
    m01 = c * e - b * f
    m02 = b * e - c * d
    m11 = a * f - c * c
    m12 = b * c - a * e
    m22 = a * d - b * b
    det = a * m00 + b * m01 + c * m02
    i00, i01, i02, i11, i12, i22 = [m / det for m in (m00, m01, m02, m11, m12, m22)]
    full = [[i00, i01, i02], [i01, i11, i12], [i02, i12, i22]]
    y = [full[q][0] * totals[6] + full[q][1] * totals[7] + full[q][2] * totals[8] for q in range(3)]
    return full, y


def cells(pj, iotac):
    half = jnp.where(pj[6:7] >= 16.0, 1.0, 0.0)
    cell_hot = jnp.where(iotac == pj[7:8] + half * PT_DEV, 1.0, 0.0).astype(BF16)
    return pj[6:7] - half * 16.0, cell_hot


def build_range(gat_ref, d_ref):
    core = lax.axis_index("pts") % 2
    first = (lax.broadcasted_iota(jnp.int32, (SLICE, OBS_DEV), 0) + core * SLICE).astype(F32)
    iotac = lax.broadcasted_iota(jnp.int32, (2 * PT_DEV, OBS_DEV), 0).astype(F32)

    def one_group(g, totals):
        x0, x1, pj = unpack(gat_ref[g])
        low, cell_hot = cells(pj, iotac)
        hot = jnp.where(first == low, 1.0, 0.0)
        left = spread(x0, x1, pj, [hot]) + stat_rows(x0, x1, pj)
        grid = nt(jnp.concatenate(left, axis=0).astype(BF16), cell_hot)
        for s in range(3):
            part = grid[s * 48 : (s + 1) * 48].astype(BF16)
            d_ref[g, :48, s * PT_DEV : (s + 1) * PT_DEV] = part[:, :PT_DEV]
            d_ref[g, 48:, s * PT_DEV : (s + 1) * PT_DEV] = part[:, PT_DEV:]
        return totals + (grid[144:176, :PT_DEV] + grid[144:176, PT_DEV:])

    return lax.fori_loop(0, N_CAM, one_group, jnp.zeros((32, PT_DEV), F32), unroll=UNROLL)


def first_kernel(gat_ref, pairs_ref, d_ref, totals_ref, near_ref):
    near_ref[...] = pairs_ref[...]
    totals_ref[...] = build_range(gat_ref, d_ref)


def fit(x):
    most = jnp.max(jnp.max(jnp.abs(x), axis=0, keepdims=True), axis=1, keepdims=True)
    power = jnp.floor(jnp.log2(jnp.maximum(most, 1e-30)))
    return power, jnp.exp2(14.0 - power)


def main_kernel(lam_ref, totals_ref, d0_ref, gat0_ref, gat1_ref, out_ref, d1_ref, w_ref):
    group = lax.axis_index("cam")
    turn = (group % 2) * 2 + lax.axis_index("pts") % 2
    gat_refs = (gat0_ref, gat1_ref)
    iota16 = lax.broadcasted_iota(jnp.int32, (16, OBS_DEV), 0).astype(F32)
    iotac = lax.broadcasted_iota(jnp.int32, (2 * PT_DEV, OBS_DEV), 0).astype(F32)
    totals = jnp.concatenate([totals_ref[...], build_range(gat1_ref, d1_ref)], axis=1)
    eight = totals[:8] + totals[8:16] + totals[16:24]
    ninth = totals[24:25] + totals[25:26] + totals[26:27]
    full, y = point_inverse([eight[i : i + 1] for i in range(8)] + [ninth], lam_ref[...])

    rhs = jnp.zeros((8, CAM_DEV), F32)
    for r in range(2):
        mine = slice(r * PT_DEV, (r + 1) * PT_DEV)
        x0, x1, pj = unpack(gat_refs[r][group])
        low, cell_hot = cells(pj, iotac)
        hot = jnp.where(iota16 == low, 1.0, 0.0)
        left = jnp.concatenate(spread(x0, x1, pj, [hot]), axis=0).astype(BF16)
        grid = nt(left, cell_hot)
        for t in range(3):
            scale = [jnp.concatenate([full[s][t][:, mine]] * 2, axis=1) for s in range(3)]
            value = (grid[:96] * scale[0] + grid[96:192] * scale[1] + grid[192:] * scale[2]).astype(BF16)
            at = t * PT_DEV
            for k in range(6):
                for h in range(2):
                    w_ref[r, k * 32 + h * 16 : k * 32 + (h + 1) * 16, at : at + PT_DEV] = (
                        value[k * 16 : (k + 1) * 16, h * PT_DEV : (h + 1) * PT_DEV])
        y8 = jnp.concatenate([v[:, mine] for v in y] + [jnp.zeros((5, PT_DEV), F32)], axis=0)
        y8 = jnp.concatenate([y8, y8], axis=1)
        y_obs = nn(jnp.concatenate(split3(y8), axis=0).astype(BF16), cell_hot)
        y_obs = y_obs[:8] + y_obs[8:16] + y_obs[16:24]
        left0 = x1[6:7] - (pj[0:1] * y_obs[0:1] + pj[1:2] * y_obs[1:2] + pj[2:3] * y_obs[2:3])
        left1 = x1[7:8] - (pj[3:4] * y_obs[0:1] + pj[4:5] * y_obs[1:2] + pj[5:6] * y_obs[2:3])
        terms = x0 * left0 + x1 * left1
        cam_hot = jnp.where(iotac[:CAM_DEV] == pj[6:7], 1.0, 0.0).astype(BF16)
        part = nt(jnp.concatenate(split3(terms), axis=0).astype(BF16), cam_hot)
        rhs = rhs + (part[:8] + part[8:16] + part[16:24])

    product = nt(d0_ref[...].reshape(N_CAM * 96, 384), w_ref[0])
    product = product + nt(d1_ref[...].reshape(N_CAM * 96, 384), w_ref[1])
    power, scale = fit(product)
    rhs_power, rhs_scale = fit(rhs)
    rhs = rhs * rhs_scale
    rhs_high = rhs.astype(BF16).astype(F32)
    rhs_rows = jnp.concatenate(
        [rhs_high, rhs - rhs_high, jnp.broadcast_to(power, (8, 32)), jnp.broadcast_to(rhs_power, (8, 32))],
        axis=1,
    )
    for i in range(2 * N_CAM):
        block = product[i * 48 : (i + 1) * 48] * scale
        tail = block[:, 128:192]
        tail = jnp.concatenate([tail[:24], tail[24:]], axis=1)
        places = [order.index(i) for order in ORDERS]
        at = jnp.where(turn < 2, jnp.where(turn == 0, places[0], places[1]), jnp.where(turn == 2, places[2], places[3]))
        out_ref[at] = jnp.concatenate([block[:, :128], tail, rhs_rows], axis=0)


def last_kernel(got_ref, pairs_ref, schur_ref, rhs_ref):
    total = jnp.zeros((72, 128), F32)
    rhs = jnp.zeros((8, CAM_DEV), F32)
    for i in range(got_ref.shape[0]):
        part = got_ref[i].astype(F32)
        scales = jnp.exp2(part[72:73] - 14.0)
        total = total + part[:72] * scales[:, 64:65]
        rhs = rhs + (part[72:80, :32] + part[72:80, 32:64]) * scales[:, 96:97]
    rhs_ref[...] = rhs[:6]
    tail = total[48:72]
    tail = jnp.concatenate([tail[:, :64], tail[:, 64:]], axis=0)
    tail = jnp.concatenate([tail, jnp.zeros((48, 64), F32)], axis=1)
    pairs = pairs_ref[...]
    left = (pairs[0:1] & (CAM_DEV - 1))
    right = (pairs[1:2] & (SLICE - 1))
    lefts = jnp.concatenate([left + CAM_DEV * k for k in range(4)], axis=1)
    rights = jnp.concatenate([right] * 6, axis=1)
    pick = jnp.where(
        lax.broadcasted_iota(jnp.int32, (128, 256), 0) == lefts, 1.0, 0.0
    ).astype(BF16)
    first = nn(jnp.concatenate(split3(total[:48]), axis=0).astype(BF16), pick)
    second = nn(jnp.concatenate(split3(tail), axis=0).astype(BF16), pick[:, :128])
    z = jnp.concatenate([first, second], axis=1)
    z = z[:48] + z[48:96] + z[96:]
    keep = lax.broadcasted_iota(jnp.int32, (SLICE, 384), 0) == rights
    rows = [
        jnp.sum(jnp.where(keep, z[l * 8 : (l + 1) * 8], 0.0), axis=0, keepdims=True) for l in range(6)
    ]
    rows = jnp.concatenate(rows, axis=0)
    for k in range(6):
        schur_ref[k * 6 : (k + 1) * 6, :] = rows[:, k * PAIR_DEV : (k + 1) * PAIR_DEV]


def local(cam_jac, pt_jac, resid, obs_cam, obs_pt, pairs, damping):
    vmem = pl.BlockSpec(memory_space=pltpu.VMEM)
    def rows(x, at):
        return jnp.pad(x, ((at, 24 - at - x.shape[0]), (0, 0)))

    cell = lax.broadcasted_iota(jnp.int32, (24, OBS_DEV), 0) * OBS_DEV
    cell = cell + lax.broadcasted_iota(jnp.int32, (24, OBS_DEV), 1)

    def code(x, mask, at):
        keep = jnp.where((cell >= at * OBS_DEV) & (cell < (at + 1) * OBS_DEV), mask, 0)
        return lax.broadcast_in_dim(x, (24, OBS_DEV), (1,)) & keep

    cam = code(obs_cam, CAM_DEV - 1, 22)
    pt = code(obs_pt, PT_DEV - 1, 23)
    second = rows(resid, 14)
    packed = ((rows(cam_jac, 0) + rows(pt_jac, 16)).astype(F32) + (cam + pt).astype(F32) + rows(resid, 12)
              + (second - lax.reduce_precision(second, 8, 7))).astype(BF16)
    packed = jnp.broadcast_to(packed[None], (N_CAM, 24, OBS_DEV))
    gathered = lax.all_to_all(packed, "cam", 0, 0)
    other = lax.ppermute(gathered, "pts", [(i, i ^ 1) for i in range(N_PTS)])
    d0, totals, near = pl.pallas_call(
        first_kernel,
        out_shape=(
            jax.ShapeDtypeStruct((N_CAM, 96, 384), BF16),
            jax.ShapeDtypeStruct((32, PT_DEV), F32),
            jax.ShapeDtypeStruct((2, PAIR_DEV), jnp.int32),
        ),
        in_specs=[vmem] * 2,
        out_specs=(vmem,) * 3,
        compiler_params=SMALL,
        cost_estimate=pl.CostEstimate(flops=10**9, bytes_accessed=10**6, transcendentals=0),
    )(gathered, pairs)
    send = pl.pallas_call(
        main_kernel,
        out_shape=jax.ShapeDtypeStruct((2 * N_CAM, ROWS, 128), F32),
        in_specs=[vmem] * 5,
        out_specs=vmem,
        compiler_params=SMALL,
        scratch_shapes=SCRATCH,
    )(damping.reshape(1, 1), totals, d0, gathered, other)
    same = [[g * N_PTS + 2 * i + c for i in ORDERS[g % 2 * 2 + c]] for g in range(N_CAM) for c in range(2)]
    got = lax.all_to_all(send.astype(jnp.float16), ("cam", "pts"), 0, 0, axis_index_groups=same).astype(F32)
    return pl.pallas_call(
        last_kernel,
        out_shape=(
            jax.ShapeDtypeStruct((36, PAIR_DEV), F32),
            jax.ShapeDtypeStruct((6, CAM_DEV), F32),
        ),
        in_specs=[vmem, vmem],
        out_specs=(vmem, vmem),
        compiler_params=SMALL,
    )(got, near)


def solution(mesh):
    return jax.shard_map(
        local,
        mesh=mesh,
        in_specs=(
            P(None, ("cam", "pts")),
            P(None, ("cam", "pts")),
            P(None, ("cam", "pts")),
            P(("cam", "pts")),
            P(("cam", "pts")),
            P(None, ("cam", "pts")),
            P(),
        ),
        out_specs=(P(None, ("cam", "pts")), P(None, "cam")),
        check_vma=False,
    )
```

```python
import jax
import jax.numpy as jnp
from jax import lax
from jax.experimental import pallas as pl
from jax.experimental.pallas import tpu as pltpu
from jax.sharding import PartitionSpec as P

CAM_DEV = 32
PT_DEV = 128
OBS_DEV = 512
PAIR_DEV = 64
N_CAM = 8
N_PTS = 32
SLICE = 8
ROWS = 80
F32 = jnp.float32
BF16 = jnp.bfloat16
UNROLL = 8
ORDERS = ([4 * ((k + 0) % 4) + (k // 4 + 0) % 4 for k in range(16)], [4 * ((k + 2) % 4) + (k // 4 + 2) % 4 for k in range(16)], [4 * ((k + 1) % 4) + (k // 4 + 1) % 4 for k in range(16)], [4 * ((k + 3) % 4) + (k // 4 + 3) % 4 for k in range(16)])
SMALL = pltpu.CompilerParams(vmem_limit_bytes=16 * 1024 * 1024)
SCRATCH = [pltpu.VMEM((N_CAM, 96, 384), BF16), pltpu.VMEM((2, 192, 384), BF16)]


def split3(x):
    hi = x.astype(BF16)
    rest = x - hi.astype(F32)
    mid = rest.astype(BF16)
    low = (rest - mid.astype(F32)).astype(BF16)
    return hi.astype(F32), mid.astype(F32), low.astype(F32)


def nt(a, b):
    return lax.dot_general(a, b, (((1,), (1,)), ((), ())), preferred_element_type=F32)


def nn(a, b):
    return lax.dot_general(a, b, (((1,), (0,)), ((), ())), preferred_element_type=F32)


def pack_kernel(cj_ref, pj_ref, res_ref, cam_ref, pt_ref, out_ref):
    cj = cj_ref[...].astype(F32)
    pj = pj_ref[...].astype(F32)
    res = res_ref[...]
    high = res.astype(BF16).astype(F32)
    low = res - high
    cam = (cam_ref[...] & (CAM_DEV - 1)).astype(F32)
    pt = (pt_ref[...] & (PT_DEV - 1)).astype(F32)
    left = jnp.concatenate([cj[:6], high, cj[6:], low], axis=0).astype(BF16)
    right = jnp.concatenate([pj, cam, pt], axis=0)
    right = jnp.concatenate([right[:, :256], right[:, 256:]], axis=0).astype(BF16)
    for g in range(N_CAM):
        out_ref[g, :, :OBS_DEV] = left
        out_ref[g, :, OBS_DEV:] = right


def unpack(m):
    x = m.astype(F32)
    x1 = jnp.concatenate([x[6:12], x[12:14] + x[14:16]], axis=0)
    return x[:8], x1, x[16:24]


def spread(x0, x1, pj, hots):
    blocks = []
    for s in range(3):
        e = x0 * pj[s : s + 1] + x1 * pj[3 + s : 4 + s]
        for hot in hots:
            for k in range(6):
                blocks.append(hot * e[k : k + 1])
    return blocks


def stat_rows(x0, x1, pj):
    jp = [pj[i : i + 1] for i in range(6)]
    r0 = x1[6:7]
    r1 = x1[7:8]
    rows = [jp[s] * jp[t] + jp[3 + s] * jp[3 + t] for s, t in
            ((0, 0), (0, 1), (0, 2), (1, 1), (1, 2), (2, 2))]
    rows = rows + [jp[s] * r0 + jp[3 + s] * r1 for s in range(3)]
    last = jnp.concatenate(list(split3(rows[8])) + [jnp.zeros((5, OBS_DEV), F32)], axis=0)
    return list(split3(jnp.concatenate(rows[:8], axis=0))) + [last]


def point_inverse(totals, lam):
    a = totals[0] + lam
    b = totals[1]
    c = totals[2]
    d = totals[3] + lam
    e = totals[4]
    f = totals[5] + lam
    m00 = d * f - e * e
    m01 = c * e - b * f
    m02 = b * e - c * d
    m11 = a * f - c * c
    m12 = b * c - a * e
    m22 = a * d - b * b
    det = a * m00 + b * m01 + c * m02
    i00, i01, i02, i11, i12, i22 = [m / det for m in (m00, m01, m02, m11, m12, m22)]
    full = [[i00, i01, i02], [i01, i11, i12], [i02, i12, i22]]
    y = [full[q][0] * totals[6] + full[q][1] * totals[7] + full[q][2] * totals[8] for q in range(3)]
    return full, y


def cells(pj, iotac):
    half = jnp.where(pj[6:7] >= 16.0, 1.0, 0.0)
    cell_hot = jnp.where(iotac == pj[7:8] + half * PT_DEV, 1.0, 0.0).astype(BF16)
    return pj[6:7] - half * 16.0, cell_hot


def place(group, core):
    at = jnp.where(group % 2 == 0, group // 2, N_CAM - 1 - group // 2)
    return jnp.where(core == 0, at, N_CAM - 1 - at)


def build_range(gat_ref, d_ref, owner):
    core = lax.axis_index("pts") % 2
    first = (lax.broadcasted_iota(jnp.int32, (SLICE, OBS_DEV), 0) + core * SLICE).astype(F32)
    iotac = lax.broadcasted_iota(jnp.int32, (2 * PT_DEV, OBS_DEV), 0).astype(F32)

    def one_group(g, totals):
        x0, x1, pj = unpack(gat_ref[place(g, owner)])
        low, cell_hot = cells(pj, iotac)
        hot = jnp.where(first == low, 1.0, 0.0)
        left = spread(x0, x1, pj, [hot]) + stat_rows(x0, x1, pj)
        grid = nt(jnp.concatenate(left, axis=0).astype(BF16), cell_hot)
        for s in range(3):
            part = grid[s * 48 : (s + 1) * 48].astype(BF16)
            d_ref[g, :48, s * PT_DEV : (s + 1) * PT_DEV] = part[:, :PT_DEV]
            d_ref[g, 48:, s * PT_DEV : (s + 1) * PT_DEV] = part[:, PT_DEV:]
        return totals + (grid[144:176, :PT_DEV] + grid[144:176, PT_DEV:])

    return lax.fori_loop(0, N_CAM, one_group, jnp.zeros((32, PT_DEV), F32), unroll=UNROLL)


def first_kernel(gat_ref, pairs_ref, d_ref, totals_ref, near_ref):
    near_ref[...] = pairs_ref[...]
    totals_ref[...] = build_range(gat_ref, d_ref, lax.axis_index("pts") % 2)


def fit(x):
    most = jnp.max(jnp.max(jnp.abs(x), axis=0, keepdims=True), axis=1, keepdims=True)
    power = jnp.floor(jnp.log2(jnp.maximum(most, 1e-30)))
    return power, jnp.exp2(14.0 - power)


def main_kernel(lam_ref, totals_ref, d0_ref, gat0_ref, gat1_ref, out_ref, d1_ref, w_ref):
    group = lax.axis_index("cam")
    core = lax.axis_index("pts") % 2
    turn = (group % 2) * 2 + core
    gat_refs = (gat0_ref, gat1_ref)
    iota16 = lax.broadcasted_iota(jnp.int32, (16, OBS_DEV), 0).astype(F32)
    iotac = lax.broadcasted_iota(jnp.int32, (2 * PT_DEV, OBS_DEV), 0).astype(F32)
    totals = jnp.concatenate([totals_ref[...], build_range(gat1_ref, d1_ref, 1 - core)], axis=1)
    eight = totals[:8] + totals[8:16] + totals[16:24]
    ninth = totals[24:25] + totals[25:26] + totals[26:27]
    full, y = point_inverse([eight[i : i + 1] for i in range(8)] + [ninth], lam_ref[...])

    rhs = jnp.zeros((8, CAM_DEV), F32)
    for r in range(2):
        mine = slice(r * PT_DEV, (r + 1) * PT_DEV)
        x0, x1, pj = unpack(gat_refs[r][place(group, core if r == 0 else 1 - core)])
        low, cell_hot = cells(pj, iotac)
        hot = jnp.where(iota16 == low, 1.0, 0.0)
        left = jnp.concatenate(spread(x0, x1, pj, [hot]), axis=0).astype(BF16)
        grid = nt(left, cell_hot)
        for t in range(3):
            scale = [jnp.concatenate([full[s][t][:, mine]] * 2, axis=1) for s in range(3)]
            value = (grid[:96] * scale[0] + grid[96:192] * scale[1] + grid[192:] * scale[2]).astype(BF16)
            at = t * PT_DEV
            for k in range(6):
                for h in range(2):
                    w_ref[r, k * 32 + h * 16 : k * 32 + (h + 1) * 16, at : at + PT_DEV] = (
                        value[k * 16 : (k + 1) * 16, h * PT_DEV : (h + 1) * PT_DEV])
        y8 = jnp.concatenate([v[:, mine] for v in y] + [jnp.zeros((5, PT_DEV), F32)], axis=0)
        y8 = jnp.concatenate([y8, y8], axis=1)
        y_obs = nn(jnp.concatenate(split3(y8), axis=0).astype(BF16), cell_hot)
        y_obs = y_obs[:8] + y_obs[8:16] + y_obs[16:24]
        left0 = x1[6:7] - (pj[0:1] * y_obs[0:1] + pj[1:2] * y_obs[1:2] + pj[2:3] * y_obs[2:3])
        left1 = x1[7:8] - (pj[3:4] * y_obs[0:1] + pj[4:5] * y_obs[1:2] + pj[5:6] * y_obs[2:3])
        terms = x0 * left0 + x1 * left1
        cam_hot = jnp.where(iotac[:CAM_DEV] == pj[6:7], 1.0, 0.0).astype(BF16)
        part = nt(jnp.concatenate(split3(terms), axis=0).astype(BF16), cam_hot)
        rhs = rhs + (part[:8] + part[8:16] + part[16:24])

    product = nt(d0_ref[...].reshape(N_CAM * 96, 384), w_ref[0])
    product = product + nt(d1_ref[...].reshape(N_CAM * 96, 384), w_ref[1])
    power, scale = fit(product)
    rhs_power, rhs_scale = fit(rhs)
    rhs = rhs * rhs_scale
    rhs_high = rhs.astype(BF16).astype(F32)
    rhs_rows = jnp.concatenate(
        [rhs_high, rhs - rhs_high, jnp.broadcast_to(power, (8, 32)), jnp.broadcast_to(rhs_power, (8, 32))],
        axis=1,
    )
    for i in range(2 * N_CAM):
        block = product[i * 48 : (i + 1) * 48] * scale
        tail = block[:, 128:192]
        tail = jnp.concatenate([tail[:24], tail[24:]], axis=1)
        places = [order.index(i) for order in ORDERS]
        at = jnp.where(turn < 2, jnp.where(turn == 0, places[0], places[1]), jnp.where(turn == 2, places[2], places[3]))
        out_ref[at] = jnp.concatenate([block[:, :128], tail, rhs_rows], axis=0)


def last_kernel(got_ref, pairs_ref, schur_ref, rhs_ref):
    total = jnp.zeros((72, 128), F32)
    rhs = jnp.zeros((8, CAM_DEV), F32)
    for i in range(got_ref.shape[0]):
        part = got_ref[i].astype(F32)
        scales = jnp.exp2(part[72:73] - 14.0)
        total = total + part[:72] * scales[:, 64:65]
        rhs = rhs + (part[72:80, :32] + part[72:80, 32:64]) * scales[:, 96:97]
    rhs_ref[...] = rhs[:6]
    tail = total[48:72]
    tail = jnp.concatenate([tail[:, :64], tail[:, 64:]], axis=0)
    tail = jnp.concatenate([tail, jnp.zeros((48, 64), F32)], axis=1)
    pairs = pairs_ref[...]
    left = (pairs[0:1] & (CAM_DEV - 1))
    right = (pairs[1:2] & (SLICE - 1))
    lefts = jnp.concatenate([left + CAM_DEV * k for k in range(4)], axis=1)
    rights = jnp.concatenate([right] * 6, axis=1)
    pick = jnp.where(
        lax.broadcasted_iota(jnp.int32, (128, 256), 0) == lefts, 1.0, 0.0
    ).astype(BF16)
    first = nn(jnp.concatenate(split3(total[:48]), axis=0).astype(BF16), pick)
    second = nn(jnp.concatenate(split3(tail), axis=0).astype(BF16), pick[:, :128])
    z = jnp.concatenate([first, second], axis=1)
    z = z[:48] + z[48:96] + z[96:]
    keep = lax.broadcasted_iota(jnp.int32, (SLICE, 384), 0) == rights
    rows = [
        jnp.sum(jnp.where(keep, z[l * 8 : (l + 1) * 8], 0.0), axis=0, keepdims=True) for l in range(6)
    ]
    rows = jnp.concatenate(rows, axis=0)
    for k in range(6):
        schur_ref[k * 6 : (k + 1) * 6, :] = rows[:, k * PAIR_DEV : (k + 1) * PAIR_DEV]


def local(cam_jac, pt_jac, resid, obs_cam, obs_pt, pairs, damping):
    vmem = pl.BlockSpec(memory_space=pltpu.VMEM)
    def rows(x, at):
        return jnp.pad(x, ((at, 24 - at - x.shape[0]), (0, 0)))

    cell = lax.broadcasted_iota(jnp.int32, (24, OBS_DEV), 0) * OBS_DEV
    cell = cell + lax.broadcasted_iota(jnp.int32, (24, OBS_DEV), 1)

    def code(x, mask, at):
        keep = jnp.where((cell >= at * OBS_DEV) & (cell < (at + 1) * OBS_DEV), mask, 0)
        return lax.broadcast_in_dim(x, (24, OBS_DEV), (1,)) & keep

    cam = code(obs_cam, CAM_DEV - 1, 22)
    pt = code(obs_pt, PT_DEV - 1, 23)
    second = rows(resid, 14)
    packed = ((rows(cam_jac, 0) + rows(pt_jac, 16)).astype(F32) + (cam + pt).astype(F32) + rows(resid, 12)
              + (second - lax.reduce_precision(second, 8, 7))).astype(BF16)
    packed = jnp.broadcast_to(packed[None], (N_CAM, 24, OBS_DEV))
    ring = [0, 2, 4, 6, 7, 5, 3, 1]
    rings = [[g * N_PTS + p for g in (ring if p % 2 == 0 else ring[::-1])] for p in range(N_PTS)]
    gathered = lax.all_to_all(packed, ("cam", "pts"), 0, 0, axis_index_groups=rings)
    other = lax.ppermute(gathered, "pts", [(i, i ^ 1) for i in range(N_PTS)])
    d0, totals, near = pl.pallas_call(
        first_kernel,
        out_shape=(
            jax.ShapeDtypeStruct((N_CAM, 96, 384), BF16),
            jax.ShapeDtypeStruct((32, PT_DEV), F32),
            jax.ShapeDtypeStruct((2, PAIR_DEV), jnp.int32),
        ),
        in_specs=[vmem] * 2,
        out_specs=(vmem,) * 3,
        compiler_params=SMALL,
        cost_estimate=pl.CostEstimate(flops=10**9, bytes_accessed=10**6, transcendentals=0),
    )(gathered, pairs)
    send = pl.pallas_call(
        main_kernel,
        out_shape=jax.ShapeDtypeStruct((2 * N_CAM, ROWS, 128), F32),
        in_specs=[vmem] * 5,
        out_specs=vmem,
        compiler_params=SMALL,
        scratch_shapes=SCRATCH,
    )(damping.reshape(1, 1), totals, d0, gathered, other)
    same = [[g * N_PTS + 2 * i + c for i in ORDERS[g % 2 * 2 + c]] for g in range(N_CAM) for c in range(2)]
    got = lax.all_to_all(send.astype(jnp.float16), ("cam", "pts"), 0, 0, axis_index_groups=same).astype(F32)
    return pl.pallas_call(
        last_kernel,
        out_shape=(
            jax.ShapeDtypeStruct((36, PAIR_DEV), F32),
            jax.ShapeDtypeStruct((6, CAM_DEV), F32),
        ),
        in_specs=[vmem, vmem],
        out_specs=(vmem, vmem),
        compiler_params=SMALL,
    )(got, near)


def solution(mesh):
    return jax.shard_map(
        local,
        mesh=mesh,
        in_specs=(
            P(None, ("cam", "pts")),
            P(None, ("cam", "pts")),
            P(None, ("cam", "pts")),
            P(("cam", "pts")),
            P(("cam", "pts")),
            P(None, ("cam", "pts")),
            P(),
        ),
        out_specs=(P(None, ("cam", "pts")), P(None, "cam")),
        check_vma=False,
    )
```

```python
import jax
import jax.numpy as jnp
from jax import lax
from jax.experimental import pallas as pl
from jax.experimental.pallas import tpu as pltpu
from jax.sharding import PartitionSpec as P

CAM_DEV = 32
PT_DEV = 128
OBS_DEV = 512
PAIR_DEV = 64
N_CAM = 8
N_PTS = 32
SLICE = 8
ROWS = 80
F32 = jnp.float32
BF16 = jnp.bfloat16
UNROLL = 8
ORDERS = ([4 * ((k + 0) % 4) + (k // 4 + 0) % 4 for k in range(16)], [4 * ((k + 2) % 4) + (k // 4 + 2) % 4 for k in range(16)], [4 * ((k + 1) % 4) + (k // 4 + 1) % 4 for k in range(16)], [4 * ((k + 3) % 4) + (k // 4 + 3) % 4 for k in range(16)])
SMALL = pltpu.CompilerParams(vmem_limit_bytes=16 * 1024 * 1024)
SCRATCH = [pltpu.VMEM((N_CAM, 96, 384), BF16), pltpu.VMEM((2, 192, 384), BF16)]


def split3(x):
    hi = x.astype(BF16)
    rest = x - hi.astype(F32)
    mid = rest.astype(BF16)
    low = (rest - mid.astype(F32)).astype(BF16)
    return hi.astype(F32), mid.astype(F32), low.astype(F32)


def nt(a, b):
    return lax.dot_general(a, b, (((1,), (1,)), ((), ())), preferred_element_type=F32)


def nn(a, b):
    return lax.dot_general(a, b, (((1,), (0,)), ((), ())), preferred_element_type=F32)


def pack_kernel(cj_ref, pj_ref, res_ref, cam_ref, pt_ref, out_ref):
    cj = cj_ref[...].astype(F32)
    pj = pj_ref[...].astype(F32)
    res = res_ref[...]
    high = res.astype(BF16).astype(F32)
    low = res - high
    cam = (cam_ref[...] & (CAM_DEV - 1)).astype(F32)
    pt = (pt_ref[...] & (PT_DEV - 1)).astype(F32)
    left = jnp.concatenate([cj[:6], high, cj[6:], low], axis=0).astype(BF16)
    right = jnp.concatenate([pj, cam, pt], axis=0)
    right = jnp.concatenate([right[:, :256], right[:, 256:]], axis=0).astype(BF16)
    for g in range(N_CAM):
        out_ref[g, :, :OBS_DEV] = left
        out_ref[g, :, OBS_DEV:] = right


def unpack(m):
    x = m.astype(F32)
    x1 = jnp.concatenate([x[6:12], x[12:14] + x[14:16]], axis=0)
    return x[:8], x1, x[16:24]


def spread(x0, x1, pj, hots):
    blocks = []
    for s in range(3):
        e = x0 * pj[s : s + 1] + x1 * pj[3 + s : 4 + s]
        for hot in hots:
            for k in range(6):
                blocks.append(hot * e[k : k + 1])
    return blocks


def stat_rows(x0, x1, pj):
    jp = [pj[i : i + 1] for i in range(6)]
    r0 = x1[6:7]
    r1 = x1[7:8]
    rows = [jp[s] * jp[t] + jp[3 + s] * jp[3 + t] for s, t in
            ((0, 0), (0, 1), (0, 2), (1, 1), (1, 2), (2, 2))]
    rows = rows + [jp[s] * r0 + jp[3 + s] * r1 for s in range(3)]
    last = jnp.concatenate(list(split3(rows[8])) + [jnp.zeros((5, OBS_DEV), F32)], axis=0)
    return list(split3(jnp.concatenate(rows[:8], axis=0))) + [last]


def point_inverse(totals, lam):
    a = totals[0] + lam
    b = totals[1]
    c = totals[2]
    d = totals[3] + lam
    e = totals[4]
    f = totals[5] + lam
    m00 = d * f - e * e
    m01 = c * e - b * f
    m02 = b * e - c * d
    m11 = a * f - c * c
    m12 = b * c - a * e
    m22 = a * d - b * b
    det = a * m00 + b * m01 + c * m02
    i00, i01, i02, i11, i12, i22 = [m / det for m in (m00, m01, m02, m11, m12, m22)]
    full = [[i00, i01, i02], [i01, i11, i12], [i02, i12, i22]]
    y = [full[q][0] * totals[6] + full[q][1] * totals[7] + full[q][2] * totals[8] for q in range(3)]
    return full, y


def cells(pj, iotac):
    half = jnp.where(pj[6:7] >= 16.0, 1.0, 0.0)
    cell_hot = jnp.where(iotac == pj[7:8] + half * PT_DEV, 1.0, 0.0).astype(BF16)
    return pj[6:7] - half * 16.0, cell_hot


def place(group, core):
    return (group + 4 * core) % N_CAM


def build_range(gat_ref, d_ref, owner):
    core = lax.axis_index("pts") % 2
    first = (lax.broadcasted_iota(jnp.int32, (SLICE, OBS_DEV), 0) + core * SLICE).astype(F32)
    iotac = lax.broadcasted_iota(jnp.int32, (2 * PT_DEV, OBS_DEV), 0).astype(F32)

    def one_group(g, totals):
        x0, x1, pj = unpack(gat_ref[place(g, owner)])
        low, cell_hot = cells(pj, iotac)
        hot = jnp.where(first == low, 1.0, 0.0)
        left = spread(x0, x1, pj, [hot]) + stat_rows(x0, x1, pj)
        grid = nt(jnp.concatenate(left, axis=0).astype(BF16), cell_hot)
        for s in range(3):
            part = grid[s * 48 : (s + 1) * 48].astype(BF16)
            d_ref[g, :48, s * PT_DEV : (s + 1) * PT_DEV] = part[:, :PT_DEV]
            d_ref[g, 48:, s * PT_DEV : (s + 1) * PT_DEV] = part[:, PT_DEV:]
        return totals + (grid[144:176, :PT_DEV] + grid[144:176, PT_DEV:])

    return lax.fori_loop(0, N_CAM, one_group, jnp.zeros((32, PT_DEV), F32), unroll=UNROLL)


def first_kernel(gat_ref, pairs_ref, d_ref, totals_ref, near_ref):
    near_ref[...] = pairs_ref[...]
    totals_ref[...] = build_range(gat_ref, d_ref, lax.axis_index("pts") % 2)


def fit(x):
    most = jnp.max(jnp.max(jnp.abs(x), axis=0, keepdims=True), axis=1, keepdims=True)
    power = jnp.floor(jnp.log2(jnp.maximum(most, 1e-30)))
    return power, jnp.exp2(14.0 - power)


def main_kernel(lam_ref, totals_ref, d0_ref, gat0_ref, gat1_ref, out_ref, d1_ref, w_ref):
    group = lax.axis_index("cam")
    core = lax.axis_index("pts") % 2
    turn = (group % 2) * 2 + core
    gat_refs = (gat0_ref, gat1_ref)
    iota16 = lax.broadcasted_iota(jnp.int32, (16, OBS_DEV), 0).astype(F32)
    iotac = lax.broadcasted_iota(jnp.int32, (2 * PT_DEV, OBS_DEV), 0).astype(F32)
    totals = jnp.concatenate([totals_ref[...], build_range(gat1_ref, d1_ref, 1 - core)], axis=1)
    eight = totals[:8] + totals[8:16] + totals[16:24]
    ninth = totals[24:25] + totals[25:26] + totals[26:27]
    full, y = point_inverse([eight[i : i + 1] for i in range(8)] + [ninth], lam_ref[...])

    rhs = jnp.zeros((8, CAM_DEV), F32)
    for r in range(2):
        mine = slice(r * PT_DEV, (r + 1) * PT_DEV)
        x0, x1, pj = unpack(gat_refs[r][place(group, core if r == 0 else 1 - core)])
        low, cell_hot = cells(pj, iotac)
        hot = jnp.where(iota16 == low, 1.0, 0.0)
        left = jnp.concatenate(spread(x0, x1, pj, [hot]), axis=0).astype(BF16)
        grid = nt(left, cell_hot)
        for t in range(3):
            scale = [jnp.concatenate([full[s][t][:, mine]] * 2, axis=1) for s in range(3)]
            value = (grid[:96] * scale[0] + grid[96:192] * scale[1] + grid[192:] * scale[2]).astype(BF16)
            at = t * PT_DEV
            for k in range(6):
                for h in range(2):
                    w_ref[r, k * 32 + h * 16 : k * 32 + (h + 1) * 16, at : at + PT_DEV] = (
                        value[k * 16 : (k + 1) * 16, h * PT_DEV : (h + 1) * PT_DEV])
        y8 = jnp.concatenate([v[:, mine] for v in y] + [jnp.zeros((5, PT_DEV), F32)], axis=0)
        y8 = jnp.concatenate([y8, y8], axis=1)
        y_obs = nn(jnp.concatenate(split3(y8), axis=0).astype(BF16), cell_hot)
        y_obs = y_obs[:8] + y_obs[8:16] + y_obs[16:24]
        left0 = x1[6:7] - (pj[0:1] * y_obs[0:1] + pj[1:2] * y_obs[1:2] + pj[2:3] * y_obs[2:3])
        left1 = x1[7:8] - (pj[3:4] * y_obs[0:1] + pj[4:5] * y_obs[1:2] + pj[5:6] * y_obs[2:3])
        terms = x0 * left0 + x1 * left1
        cam_hot = jnp.where(iotac[:CAM_DEV] == pj[6:7], 1.0, 0.0).astype(BF16)
        part = nt(jnp.concatenate(split3(terms), axis=0).astype(BF16), cam_hot)
        rhs = rhs + (part[:8] + part[8:16] + part[16:24])

    product = nt(d0_ref[...].reshape(N_CAM * 96, 384), w_ref[0])
    product = product + nt(d1_ref[...].reshape(N_CAM * 96, 384), w_ref[1])
    power, scale = fit(product)
    rhs_power, rhs_scale = fit(rhs)
    rhs = rhs * rhs_scale
    rhs_high = rhs.astype(BF16).astype(F32)
    rhs_rows = jnp.concatenate(
        [rhs_high, rhs - rhs_high, jnp.broadcast_to(power, (8, 32)), jnp.broadcast_to(rhs_power, (8, 32))],
        axis=1,
    )
    for i in range(2 * N_CAM):
        block = product[i * 48 : (i + 1) * 48] * scale
        tail = block[:, 128:192]
        tail = jnp.concatenate([tail[:24], tail[24:]], axis=1)
        places = [order.index(i) for order in ORDERS]
        at = jnp.where(turn < 2, jnp.where(turn == 0, places[0], places[1]), jnp.where(turn == 2, places[2], places[3]))
        out_ref[at] = jnp.concatenate([block[:, :128], tail, rhs_rows], axis=0)


def last_kernel(got_ref, pairs_ref, schur_ref, rhs_ref):
    total = jnp.zeros((72, 128), F32)
    rhs = jnp.zeros((8, CAM_DEV), F32)
    for i in range(got_ref.shape[0]):
        part = got_ref[i].astype(F32)
        scales = jnp.exp2(part[72:73] - 14.0)
        total = total + part[:72] * scales[:, 64:65]
        rhs = rhs + (part[72:80, :32] + part[72:80, 32:64]) * scales[:, 96:97]
    rhs_ref[...] = rhs[:6]
    tail = total[48:72]
    tail = jnp.concatenate([tail[:, :64], tail[:, 64:]], axis=0)
    tail = jnp.concatenate([tail, jnp.zeros((48, 64), F32)], axis=1)
    pairs = pairs_ref[...]
    left = (pairs[0:1] & (CAM_DEV - 1))
    right = (pairs[1:2] & (SLICE - 1))
    lefts = jnp.concatenate([left + CAM_DEV * k for k in range(4)], axis=1)
    rights = jnp.concatenate([right] * 6, axis=1)
    pick = jnp.where(
        lax.broadcasted_iota(jnp.int32, (128, 256), 0) == lefts, 1.0, 0.0
    ).astype(BF16)
    first = nn(jnp.concatenate(split3(total[:48]), axis=0).astype(BF16), pick)
    second = nn(jnp.concatenate(split3(tail), axis=0).astype(BF16), pick[:, :128])
    z = jnp.concatenate([first, second], axis=1)
    z = z[:48] + z[48:96] + z[96:]
    keep = lax.broadcasted_iota(jnp.int32, (SLICE, 384), 0) == rights
    rows = [
        jnp.sum(jnp.where(keep, z[l * 8 : (l + 1) * 8], 0.0), axis=0, keepdims=True) for l in range(6)
    ]
    rows = jnp.concatenate(rows, axis=0)
    for k in range(6):
        schur_ref[k * 6 : (k + 1) * 6, :] = rows[:, k * PAIR_DEV : (k + 1) * PAIR_DEV]


def local(cam_jac, pt_jac, resid, obs_cam, obs_pt, pairs, damping):
    vmem = pl.BlockSpec(memory_space=pltpu.VMEM)
    def rows(x, at):
        return jnp.pad(x, ((at, 24 - at - x.shape[0]), (0, 0)))

    cell = lax.broadcasted_iota(jnp.int32, (24, OBS_DEV), 0) * OBS_DEV
    cell = cell + lax.broadcasted_iota(jnp.int32, (24, OBS_DEV), 1)

    def code(x, mask, at):
        keep = jnp.where((cell >= at * OBS_DEV) & (cell < (at + 1) * OBS_DEV), mask, 0)
        return lax.broadcast_in_dim(x, (24, OBS_DEV), (1,)) & keep

    cam = code(obs_cam, CAM_DEV - 1, 22)
    pt = code(obs_pt, PT_DEV - 1, 23)
    second = rows(resid, 14)
    packed = ((rows(cam_jac, 0) + rows(pt_jac, 16)).astype(F32) + (cam + pt).astype(F32) + rows(resid, 12)
              + (second - lax.reduce_precision(second, 8, 7))).astype(BF16)
    packed = jnp.broadcast_to(packed[None], (N_CAM, 24, OBS_DEV))
    ring = list(range(N_CAM))
    rings = [[g * N_PTS + p for g in (ring if p % 2 == 0 else ring[4:] + ring[:4])] for p in range(N_PTS)]
    gathered = lax.all_to_all(packed, ("cam", "pts"), 0, 0, axis_index_groups=rings)
    other = lax.ppermute(gathered, "pts", [(i, i ^ 1) for i in range(N_PTS)])
    d0, totals, near = pl.pallas_call(
        first_kernel,
        out_shape=(
            jax.ShapeDtypeStruct((N_CAM, 96, 384), BF16),
            jax.ShapeDtypeStruct((32, PT_DEV), F32),
            jax.ShapeDtypeStruct((2, PAIR_DEV), jnp.int32),
        ),
        in_specs=[vmem] * 2,
        out_specs=(vmem,) * 3,
        compiler_params=SMALL,
        cost_estimate=pl.CostEstimate(flops=10**9, bytes_accessed=10**6, transcendentals=0),
    )(gathered, pairs)
    send = pl.pallas_call(
        main_kernel,
        out_shape=jax.ShapeDtypeStruct((2 * N_CAM, ROWS, 128), F32),
        in_specs=[vmem] * 5,
        out_specs=vmem,
        compiler_params=SMALL,
        scratch_shapes=SCRATCH,
    )(damping.reshape(1, 1), totals, d0, gathered, other)
    same = [[g * N_PTS + 2 * i + c for i in ORDERS[g % 2 * 2 + c]] for g in range(N_CAM) for c in range(2)]
    got = lax.all_to_all(send.astype(jnp.float16), ("cam", "pts"), 0, 0, axis_index_groups=same).astype(F32)
    return pl.pallas_call(
        last_kernel,
        out_shape=(
            jax.ShapeDtypeStruct((36, PAIR_DEV), F32),
            jax.ShapeDtypeStruct((6, CAM_DEV), F32),
        ),
        in_specs=[vmem, vmem],
        out_specs=(vmem, vmem),
        compiler_params=SMALL,
    )(got, near)


def solution(mesh):
    return jax.shard_map(
        local,
        mesh=mesh,
        in_specs=(
            P(None, ("cam", "pts")),
            P(None, ("cam", "pts")),
            P(None, ("cam", "pts")),
            P(("cam", "pts")),
            P(("cam", "pts")),
            P(None, ("cam", "pts")),
            P(),
        ),
        out_specs=(P(None, ("cam", "pts")), P(None, "cam")),
        check_vma=False,
    )
```

```python
import jax
import jax.numpy as jnp
from jax import lax
from jax.experimental import pallas as pl
from jax.experimental.pallas import tpu as pltpu
from jax.sharding import PartitionSpec as P

CAM_DEV = 32
PT_DEV = 128
OBS_DEV = 512
PAIR_DEV = 64
N_CAM = 8
N_PTS = 32
SLICE = 8
ROWS = 80
F32 = jnp.float32
BF16 = jnp.bfloat16
UNROLL = 8
ORDERS = ([4 * ((k + 0) % 4) + (k // 4 + 0) % 4 for k in range(16)], [4 * ((k + 2) % 4) + (k // 4 + 2) % 4 for k in range(16)], [4 * ((k + 1) % 4) + (k // 4 + 1) % 4 for k in range(16)], [4 * ((k + 3) % 4) + (k // 4 + 3) % 4 for k in range(16)])
SMALL = pltpu.CompilerParams(vmem_limit_bytes=16 * 1024 * 1024)
SCRATCH = [pltpu.VMEM((N_CAM, 96, 384), BF16), pltpu.VMEM((2, 192, 384), BF16)]


def split3(x):
    hi = x.astype(BF16)
    rest = x - hi.astype(F32)
    mid = rest.astype(BF16)
    low = (rest - mid.astype(F32)).astype(BF16)
    return hi.astype(F32), mid.astype(F32), low.astype(F32)


def nt(a, b):
    return lax.dot_general(a, b, (((1,), (1,)), ((), ())), preferred_element_type=F32)


def nn(a, b):
    return lax.dot_general(a, b, (((1,), (0,)), ((), ())), preferred_element_type=F32)


def pack_kernel(cj_ref, pj_ref, res_ref, cam_ref, pt_ref, out_ref):
    cj = cj_ref[...].astype(F32)
    pj = pj_ref[...].astype(F32)
    res = res_ref[...]
    high = res.astype(BF16).astype(F32)
    low = res - high
    cam = (cam_ref[...] & (CAM_DEV - 1)).astype(F32)
    pt = (pt_ref[...] & (PT_DEV - 1)).astype(F32)
    left = jnp.concatenate([cj[:6], high, cj[6:], low], axis=0).astype(BF16)
    right = jnp.concatenate([pj, cam, pt], axis=0)
    right = jnp.concatenate([right[:, :256], right[:, 256:]], axis=0).astype(BF16)
    for g in range(N_CAM):
        out_ref[g, :, :OBS_DEV] = left
        out_ref[g, :, OBS_DEV:] = right


def unpack(m):
    x = m.astype(F32)
    x1 = jnp.concatenate([x[6:12], x[12:14] + x[14:16]], axis=0)
    return x[:8], x1, x[16:24]


def spread(x0, x1, pj, hots):
    blocks = []
    for s in range(3):
        e = x0 * pj[s : s + 1] + x1 * pj[3 + s : 4 + s]
        for hot in hots:
            for k in range(6):
                blocks.append(hot * e[k : k + 1])
    return blocks


def stat_rows(x0, x1, pj):
    jp = [pj[i : i + 1] for i in range(6)]
    r0 = x1[6:7]
    r1 = x1[7:8]
    rows = [jp[s] * jp[t] + jp[3 + s] * jp[3 + t] for s, t in
            ((0, 0), (0, 1), (0, 2), (1, 1), (1, 2), (2, 2))]
    rows = rows + [jp[s] * r0 + jp[3 + s] * r1 for s in range(3)]
    last = jnp.concatenate(list(split3(rows[8])) + [jnp.zeros((5, OBS_DEV), F32)], axis=0)
    return list(split3(jnp.concatenate(rows[:8], axis=0))) + [last]


def point_inverse(totals, lam):
    a = totals[0] + lam
    b = totals[1]
    c = totals[2]
    d = totals[3] + lam
    e = totals[4]
    f = totals[5] + lam
    m00 = d * f - e * e
    m01 = c * e - b * f
    m02 = b * e - c * d
    m11 = a * f - c * c
    m12 = b * c - a * e
    m22 = a * d - b * b
    det = a * m00 + b * m01 + c * m02
    i00, i01, i02, i11, i12, i22 = [m / det for m in (m00, m01, m02, m11, m12, m22)]
    full = [[i00, i01, i02], [i01, i11, i12], [i02, i12, i22]]
    y = [full[q][0] * totals[6] + full[q][1] * totals[7] + full[q][2] * totals[8] for q in range(3)]
    return full, y


def cells(pj, iotac):
    half = jnp.where(pj[6:7] >= 16.0, 1.0, 0.0)
    cell_hot = jnp.where(iotac == pj[7:8] + half * PT_DEV, 1.0, 0.0).astype(BF16)
    return pj[6:7] - half * 16.0, cell_hot


def place(group, core):
    return (group + 4 * core) % N_CAM


def build_range(gat_ref, d_ref, owner):
    core = lax.axis_index("pts") % 2
    first = (lax.broadcasted_iota(jnp.int32, (SLICE, OBS_DEV), 0) + core * SLICE).astype(F32)
    iotac = lax.broadcasted_iota(jnp.int32, (2 * PT_DEV, OBS_DEV), 0).astype(F32)

    def one_group(g, totals):
        x0, x1, pj = unpack(gat_ref[place(g, owner)])
        low, cell_hot = cells(pj, iotac)
        hot = jnp.where(first == low, 1.0, 0.0)
        left = spread(x0, x1, pj, [hot]) + stat_rows(x0, x1, pj)
        grid = nt(jnp.concatenate(left, axis=0).astype(BF16), cell_hot)
        for s in range(3):
            part = grid[s * 48 : (s + 1) * 48].astype(BF16)
            d_ref[g, :48, s * PT_DEV : (s + 1) * PT_DEV] = part[:, :PT_DEV]
            d_ref[g, 48:, s * PT_DEV : (s + 1) * PT_DEV] = part[:, PT_DEV:]
        return totals + (grid[144:176, :PT_DEV] + grid[144:176, PT_DEV:])

    return lax.fori_loop(0, N_CAM, one_group, jnp.zeros((32, PT_DEV), F32), unroll=UNROLL)


def first_kernel(gat_ref, pairs_ref, d_ref, totals_ref, near_ref):
    near_ref[...] = pairs_ref[...]
    totals_ref[...] = build_range(gat_ref, d_ref, lax.axis_index("pts") % 2)


def fit(x):
    most = jnp.max(jnp.max(jnp.abs(x), axis=0, keepdims=True), axis=1, keepdims=True)
    power = jnp.floor(jnp.log2(jnp.maximum(most, 1e-30)))
    return power, jnp.exp2(14.0 - power)


def main_kernel(lam_ref, totals_ref, d0_ref, gat0_ref, gat1_ref, out_ref, d1_ref, w_ref):
    group = lax.axis_index("cam")
    core = lax.axis_index("pts") % 2
    turn = (group % 2) * 2 + core
    gat_refs = (gat0_ref, gat1_ref)
    iota16 = lax.broadcasted_iota(jnp.int32, (16, OBS_DEV), 0).astype(F32)
    iotac = lax.broadcasted_iota(jnp.int32, (2 * PT_DEV, OBS_DEV), 0).astype(F32)
    totals = jnp.concatenate([totals_ref[...], build_range(gat1_ref, d1_ref, 1 - core)], axis=1)
    eight = totals[:8] + totals[8:16] + totals[16:24]
    ninth = totals[24:25] + totals[25:26] + totals[26:27]
    full, y = point_inverse([eight[i : i + 1] for i in range(8)] + [ninth], lam_ref[...])

    rhs = jnp.zeros((8, CAM_DEV), F32)
    for r in range(2):
        mine = slice(r * PT_DEV, (r + 1) * PT_DEV)
        x0, x1, pj = unpack(gat_refs[r][place(group, core if r == 0 else 1 - core)])
        low, cell_hot = cells(pj, iotac)
        hot = jnp.where(iota16 == low, 1.0, 0.0)
        left = jnp.concatenate(spread(x0, x1, pj, [hot]), axis=0).astype(BF16)
        grid = nt(left, cell_hot)
        for t in range(3):
            scale = [jnp.concatenate([full[s][t][:, mine]] * 2, axis=1) for s in range(3)]
            value = (grid[:96] * scale[0] + grid[96:192] * scale[1] + grid[192:] * scale[2]).astype(BF16)
            at = t * PT_DEV
            for k in range(6):
                for h in range(2):
                    w_ref[r, k * 32 + h * 16 : k * 32 + (h + 1) * 16, at : at + PT_DEV] = (
                        value[k * 16 : (k + 1) * 16, h * PT_DEV : (h + 1) * PT_DEV])
        y8 = jnp.concatenate([v[:, mine] for v in y] + [jnp.zeros((5, PT_DEV), F32)], axis=0)
        y8 = jnp.concatenate([y8, y8], axis=1)
        y_obs = nn(jnp.concatenate(split3(y8), axis=0).astype(BF16), cell_hot)
        y_obs = y_obs[:8] + y_obs[8:16] + y_obs[16:24]
        left0 = x1[6:7] - (pj[0:1] * y_obs[0:1] + pj[1:2] * y_obs[1:2] + pj[2:3] * y_obs[2:3])
        left1 = x1[7:8] - (pj[3:4] * y_obs[0:1] + pj[4:5] * y_obs[1:2] + pj[5:6] * y_obs[2:3])
        terms = x0 * left0 + x1 * left1
        cam_hot = jnp.where(iotac[:CAM_DEV] == pj[6:7], 1.0, 0.0).astype(BF16)
        part = nt(jnp.concatenate(split3(terms), axis=0).astype(BF16), cam_hot)
        rhs = rhs + (part[:8] + part[8:16] + part[16:24])

    product = nt(d0_ref[...].reshape(N_CAM * 96, 384), w_ref[0])
    product = product + nt(d1_ref[...].reshape(N_CAM * 96, 384), w_ref[1])
    power, scale = fit(product)
    rhs_power, rhs_scale = fit(rhs)
    rhs = rhs * rhs_scale
    rhs_high = rhs.astype(BF16).astype(F32)
    rhs_rows = jnp.concatenate(
        [rhs_high, rhs - rhs_high, jnp.broadcast_to(power, (8, 32)), jnp.broadcast_to(rhs_power, (8, 32))],
        axis=1,
    )
    for i in range(2 * N_CAM):
        block = product[i * 48 : (i + 1) * 48] * scale
        tail = block[:, 128:192]
        tail = jnp.concatenate([tail[:24], tail[24:]], axis=1)
        places = [order.index(i) for order in ORDERS]
        at = jnp.where(turn < 2, jnp.where(turn == 0, places[0], places[1]), jnp.where(turn == 2, places[2], places[3]))
        out_ref[at] = jnp.concatenate([block[:, :128], tail, rhs_rows], axis=0)


def last_kernel(got_ref, pairs_ref, schur_ref, rhs_ref):
    total = jnp.zeros((72, 128), F32)
    rhs = jnp.zeros((8, CAM_DEV), F32)
    for i in range(got_ref.shape[0]):
        part = got_ref[i].astype(F32)
        scales = jnp.exp2(part[72:73] - 14.0)
        total = total + part[:72] * scales[:, 64:65]
        rhs = rhs + (part[72:80, :32] + part[72:80, 32:64]) * scales[:, 96:97]
    rhs_ref[...] = rhs[:6]
    tail = total[48:72]
    tail = jnp.concatenate([tail[:, :64], tail[:, 64:]], axis=0)
    tail = jnp.concatenate([tail, jnp.zeros((48, 64), F32)], axis=1)
    pairs = pairs_ref[...]
    left = (pairs[0:1] & (CAM_DEV - 1))
    right = (pairs[1:2] & (SLICE - 1))
    lefts = jnp.concatenate([left + CAM_DEV * k for k in range(4)], axis=1)
    rights = jnp.concatenate([right] * 6, axis=1)
    pick = jnp.where(
        lax.broadcasted_iota(jnp.int32, (128, 256), 0) == lefts, 1.0, 0.0
    ).astype(BF16)
    both = jnp.concatenate([total[:48], tail], axis=0)
    high = both.astype(BF16)
    low = (both - high.astype(F32)).astype(BF16)
    z = nn(high, pick) + nn(low, pick)
    z = jnp.concatenate([z[:48], z[48:, :128]], axis=1)
    keep = lax.broadcasted_iota(jnp.int32, (SLICE, 384), 0) == rights
    rows = [
        jnp.sum(jnp.where(keep, z[l * 8 : (l + 1) * 8], 0.0), axis=0, keepdims=True) for l in range(6)
    ]
    rows = jnp.concatenate(rows, axis=0)
    for k in range(6):
        schur_ref[k * 6 : (k + 1) * 6, :] = rows[:, k * PAIR_DEV : (k + 1) * PAIR_DEV]


def local(cam_jac, pt_jac, resid, obs_cam, obs_pt, pairs, damping):
    vmem = pl.BlockSpec(memory_space=pltpu.VMEM)
    def rows(x, at):
        return jnp.pad(x, ((at, 24 - at - x.shape[0]), (0, 0)))

    cell = lax.broadcasted_iota(jnp.int32, (24, OBS_DEV), 0) * OBS_DEV
    cell = cell + lax.broadcasted_iota(jnp.int32, (24, OBS_DEV), 1)

    def code(x, mask, at):
        keep = jnp.where((cell >= at * OBS_DEV) & (cell < (at + 1) * OBS_DEV), mask, 0)
        return lax.broadcast_in_dim(x, (24, OBS_DEV), (1,)) & keep

    cam = code(obs_cam, CAM_DEV - 1, 22)
    pt = code(obs_pt, PT_DEV - 1, 23)
    second = rows(resid, 14)
    packed = ((rows(cam_jac, 0) + rows(pt_jac, 16)).astype(F32) + (cam + pt).astype(F32) + rows(resid, 12)
              + (second - lax.reduce_precision(second, 8, 7))).astype(BF16)
    packed = jnp.broadcast_to(packed[None], (N_CAM, 24, OBS_DEV))
    ring = list(range(N_CAM))
    rings = [[g * N_PTS + p for g in (ring if p % 2 == 0 else ring[4:] + ring[:4])] for p in range(N_PTS)]
    gathered = lax.all_to_all(packed, ("cam", "pts"), 0, 0, axis_index_groups=rings)
    other = lax.ppermute(gathered, "pts", [(i, i ^ 1) for i in range(N_PTS)])
    d0, totals, near = pl.pallas_call(
        first_kernel,
        out_shape=(
            jax.ShapeDtypeStruct((N_CAM, 96, 384), BF16),
            jax.ShapeDtypeStruct((32, PT_DEV), F32),
            jax.ShapeDtypeStruct((2, PAIR_DEV), jnp.int32),
        ),
        in_specs=[vmem] * 2,
        out_specs=(vmem,) * 3,
        compiler_params=SMALL,
        cost_estimate=pl.CostEstimate(flops=10**9, bytes_accessed=10**6, transcendentals=0),
    )(gathered, pairs)
    send = pl.pallas_call(
        main_kernel,
        out_shape=jax.ShapeDtypeStruct((2 * N_CAM, ROWS, 128), F32),
        in_specs=[vmem] * 5,
        out_specs=vmem,
        compiler_params=SMALL,
        scratch_shapes=SCRATCH,
    )(damping.reshape(1, 1), totals, d0, gathered, other)
    same = [[g * N_PTS + 2 * i + c for i in ORDERS[g % 2 * 2 + c]] for g in range(N_CAM) for c in range(2)]
    got = lax.all_to_all(send.astype(jnp.float16), ("cam", "pts"), 0, 0, axis_index_groups=same).astype(F32)
    return pl.pallas_call(
        last_kernel,
        out_shape=(
            jax.ShapeDtypeStruct((36, PAIR_DEV), F32),
            jax.ShapeDtypeStruct((6, CAM_DEV), F32),
        ),
        in_specs=[vmem, vmem],
        out_specs=(vmem, vmem),
        compiler_params=SMALL,
    )(got, near)


def solution(mesh):
    return jax.shard_map(
        local,
        mesh=mesh,
        in_specs=(
            P(None, ("cam", "pts")),
            P(None, ("cam", "pts")),
            P(None, ("cam", "pts")),
            P(("cam", "pts")),
            P(("cam", "pts")),
            P(None, ("cam", "pts")),
            P(),
        ),
        out_specs=(P(None, ("cam", "pts")), P(None, "cam")),
        check_vma=False,
    )
```
